1024 devices in a mesh: level: 8 (over y_hi, core), block: 128 (over y_lo, x, z).
Axes of the slice: x: 4, y: 8 (y_hi: 4, y_lo: 2; y = y_hi * 2 + y_lo), z: 16, core: 2. Of those that a mesh axis runs over, the one named last changes fastest.
Arguments:
- flow_state: float32 [8, 5, 1024, 16, 128], P('level', None, 'block'), as said below
Outputs:
- updated: float32 [8, 5, 1024, 16, 128], P('level', None, 'block')
Inputs may be any that keep to these rules, and one draw needn't show every extreme that they name: `flow_state`: every cell has density between 0.5 and 2.6 and pressure between 0.35 and 1.4, and the velocity along the cells' first dimension lies between 7 and 9.
All inputs are finite; a program needn't handle non-finite values.
Results may differ from the reference program's by a relative error of at most 0.0001.
Values sent between devices are 32-bit elements; how exact they have to be, the bound alone decides.
No kernel may reach another device: no remote copies, remote signals or barrier semaphores. Data moves between devices by JAX's collectives and lax.ppermute only.
A program may use at most 32 MiB of HBM per device.

```python
import jax
import jax.numpy as jnp
from jax import lax

SWEEPS = 8
CY = 16
CZ = 128
NX = 1024
LEVELS = 8


GAMMA = 1.4


def draw_flow_state(key, part):
    grid_shape = (LEVELS, NX, CY, CZ)
    subkeys = jax.random.split(key, 5)

    def rough_field(sub):
        return jnp.clip(jax.random.normal(sub, grid_shape, jnp.float32) * 0.4, -1.0, 1.0)
    density = jnp.exp(0.69 * rough_field(subkeys[0]))
    pressure = 0.7 * jnp.exp(0.69 * rough_field(subkeys[1]))
    along = 8.0 + rough_field(subkeys[2])
    across = 0.6 * rough_field(subkeys[3])
    normal = 0.6 * rough_field(subkeys[4])
    energy = pressure / (GAMMA - 1.0) + 0.5 * density * (along * along + across * across + normal * normal)
    return jnp.stack([density, density * along, density * across, density * normal, energy], axis=1).astype(jnp.float32)


def setup_inputs(seed: int = 0) -> dict:
    keys = jax.random.split(jax.random.key(seed), 2)
    return {
        "flow_state": draw_flow_state(jax.random.fold_in(keys[1], 71), 0),
    }


GAMMA = 1.4
COURANT = 0.8
SMOOTHING = 2.0

def flux_parts(cells, direction):
    density = cells[0]
    velocity = cells[1:4] / density
    pressure = (GAMMA - 1.0) * (cells[4] - 0.5 * density * lax.optimization_barrier(jnp.sum(velocity * velocity, axis=0)))
    sound_speed = jnp.sqrt(GAMMA * pressure / density)
    normal = velocity[direction]
    momentum = cells[1:4] * normal
    momentum = momentum.at[direction].add(pressure)
    flux_vector = jnp.concatenate([cells[1 + direction][None], momentum, ((cells[4] + pressure) * normal)[None]], axis=0)
    return (flux_vector, jnp.abs(normal) + sound_speed)

def face_flux(left_state, right_state, direction):
    flux_left, speed_left = flux_parts(left_state, direction)
    flux_right, speed_right = flux_parts(right_state, direction)
    wave_speed = jnp.maximum(speed_left, speed_right)
    return 0.5 * (flux_left + flux_right) - 0.5 * wave_speed * (right_state - left_state)

def trim_others(extended, direction):
    for axis_index in range(1, 4):
        if axis_index != 1 + direction:
            extended = lax.slice_in_dim(extended, 1, extended.shape[axis_index] - 1, axis=axis_index)
    return extended

def scaled_residual(extended, refinement):
    interior = extended[:, 1:-1, 1:-1, 1:-1]
    divergence = jnp.zeros_like(interior)
    for direction in range(3):
        strip_cells = trim_others(extended, direction)
        length = strip_cells.shape[1 + direction]
        face_values = face_flux(lax.slice_in_dim(strip_cells, 0, length - 1, axis=1 + direction), lax.slice_in_dim(strip_cells, 1, length, axis=1 + direction), direction)
        difference = lax.slice_in_dim(face_values, 1, length - 1, axis=1 + direction) - lax.slice_in_dim(face_values, 0, length - 2, axis=1 + direction)
        if direction == 2:
            difference = difference * refinement
        divergence = divergence - difference
    density = interior[0]
    velocity = interior[1:4] / density
    pressure = (GAMMA - 1.0) * (interior[4] - 0.5 * density * lax.optimization_barrier(jnp.sum(velocity * velocity, axis=0)))
    sound_speed = jnp.sqrt(GAMMA * pressure / density)
    wave_rate = jnp.abs(velocity[0]) + sound_speed + (jnp.abs(velocity[1]) + sound_speed) + (jnp.abs(velocity[2]) + sound_speed) * refinement
    return COURANT * divergence / wave_rate

def transverse_sum(field):
    padded = jnp.pad(field, ((0, 0), (0, 0), (1, 1), (1, 1)))
    return padded[:, :, 2:, 1:-1] + padded[:, :, :-2, 1:-1] + padded[:, :, 1:-1, 2:] + padded[:, :, 1:-1, :-2]

def reference(flow_state):
    level_count = flow_state.shape[0]
    depth_cells = flow_state.shape[4]
    quarter = depth_cells // 4
    residuals = []
    for level_index in range(level_count):
        fields = flow_state[level_index]
        widened = jnp.pad(fields, ((0, 0), (1, 1), (1, 1), (0, 0)), mode='edge')
        if level_index == 0:
            ghosts = jnp.stack([fields[:, :, :, 0], fields[:, :, :, -1]], axis=-1)
        else:
            coarse = flow_state[level_index - 1]
            ghosts = jnp.stack([coarse[:, :, :, quarter - 1], coarse[:, :, :, 3 * quarter]], axis=-1)
        ghosts = jnp.pad(ghosts, ((0, 0), (1, 1), (1, 1), (0, 0)), mode='edge')
        extended = jnp.concatenate([ghosts[..., :1], widened, ghosts[..., 1:]], axis=3)
        residuals.append(scaled_residual(extended, jnp.float32(2 ** level_index)))
    corrections = []
    for level_index in range(level_count):
        target = residuals[level_index]
        if level_index < level_count - 1:
            finer = residuals[level_index + 1]
            covered_part = (finer[..., 0::2] + finer[..., 1::2]) * 0.5
            target = jnp.concatenate([target[..., :quarter], covered_part, target[..., 3 * quarter:]], axis=3)
        correction = jnp.zeros_like(target)
        for sweep_index in range(SWEEPS):
            widened = jnp.pad(correction, ((0, 0), (1, 1), (0, 0), (0, 0)))
            neighbours = widened[:, 2:] + widened[:, :-2] + transverse_sum(correction)
            correction = (target + SMOOTHING * neighbours) / (1.0 + 6.0 * SMOOTHING)
        corrections.append(correction)
    results = []
    for level_index in range(level_count):
        result = flow_state[level_index] + corrections[level_index]
        if level_index >= 1:
            lifted = jnp.repeat(corrections[level_index - 1][..., quarter:3 * quarter], 2, axis=3)
            result = result + lifted
        results.append(result)
    return jnp.stack(results)
```

```python
import functools

import jax
import jax.numpy as jnp
import numpy as np
from jax import lax
from jax.experimental import pallas as pl
from jax.experimental.pallas import tpu as pltpu
from jax.sharding import PartitionSpec as P

SWEEPS = 8
GAMMA = 1.4
COURANT = 0.8
SMOOTHING = 2.0
COMPS = 5
ROWS = 8
HALO = SWEEPS - 1
LATE = ROWS
EARLY = ROWS + HALO - 1
F32 = jnp.float32


def lanes(shape):
    return lax.broadcasted_iota(jnp.int32, shape, len(shape) - 1)


def sublanes(shape):
    return lax.broadcasted_iota(jnp.int32, shape, len(shape) - 2)


def lane_roll(x, shift):
    return pltpu.roll(x, shift, x.ndim - 1)


def exact_dot(x, w):
    high = x.astype(jnp.bfloat16)
    rest = x - high.astype(F32)
    mid = rest.astype(jnp.bfloat16)
    low = (rest - mid.astype(F32)).astype(jnp.bfloat16)
    dot = functools.partial(jnp.dot, preferred_element_type=F32)
    return dot(high, w) + dot(mid, w) + dot(low, w)


def primitives(q):
    inverse = 1.0 / q[0]
    v = [q[1] * inverse, q[2] * inverse, q[3] * inverse]
    pressure = (GAMMA - 1.0) * (q[4] - 0.5 * (q[1] * v[0] + q[2] * v[1] + q[3] * v[2]))
    sound = jnp.sqrt(GAMMA * pressure * inverse)
    return v, pressure, sound


def flux(q, normal, pressure, d):
    out = [q[1 + d], q[1] * normal, q[2] * normal, q[3] * normal, (q[4] + pressure) * normal]
    out[1 + d] = out[1 + d] + pressure
    return out


def face(q_left, f_left, s_left, q_right, f_right, s_right):
    speed = jnp.maximum(s_left, s_right)
    return [
        (f_left[c] + f_right[c]) - speed * (q_right[c] - q_left[c]) for c in range(COMPS)
    ]


def axis_flags():
    level = lax.axis_index("level")
    block = lax.axis_index("block")
    refinement = jnp.left_shift(jnp.int32(1), level).astype(F32)
    return level, block, refinement


def residual_kernel(
    n, upper, first_ref, second_ref, w_ref, res_ref, down_ref, up_ref, x_ref
):
    level, block, refinement = axis_flags()
    half, groups = n // 2, -(-n // 8)
    ny, nz = x_ref.shape[2:]
    if upper:
        x_ref[:, :ROWS] = first_ref[...]
        outside = (block == lax.axis_size("block") - 1).astype(jnp.int32)
        edge = jnp.broadcast_to(first_ref[:, ROWS - 1 :], first_ref.shape)
        x_ref[:, ROWS:] = jnp.where(outside == 1, edge, second_ref[...])
    else:
        x_ref[:, ROWS:] = second_ref[...]
        outside = (block == 0).astype(jnp.int32)
        edge = jnp.broadcast_to(second_ref[:, :1], first_ref.shape)
        x_ref[:, :ROWS] = jnp.where(outside == 1, edge, first_ref[...])
    lane, sub = lanes((ny, nz)), sublanes((ny, nz))
    down_ref[COMPS * half :] = jnp.zeros((2, ny, nz), F32)
    up_ref[...] = jnp.zeros(up_ref.shape, F32)

    def load(i):
        return [x_ref[c, i] for c in range(COMPS)]

    def row(i, carried):
        q, v, pressure, sound, face_low = carried
        qn = load(i + 1)
        vn, pn, sn = primitives(qn)
        face_high = face(
            q, flux(q, v[0], pressure, 0), jnp.abs(v[0]) + sound,
            qn, flux(qn, vn[0], pn, 0), jnp.abs(vn[0]) + sn,
        )
        total = [face_low[c] - face_high[c] for c in range(COMPS)]
        f = flux(q, v[1], pressure, 1)
        speed = jnp.abs(v[1]) + sound

        def below(a):
            return jnp.where(sub == 0, a, pltpu.roll(a, 1, 0))

        qb = [below(a) for a in q]
        fb = flux(qb, below(v[1]), below(pressure), 1)
        low = face(qb, fb, below(speed), q, f, speed)
        for c in range(COMPS):
            high = jnp.where(sub == ny - 1, 2.0 * f[c], pltpu.roll(low[c], ny - 1, 0))
            total[c] = total[c] + (low[c] - high)
        f = flux(q, v[2], pressure, 2)
        speed = jnp.abs(v[2]) + sound
        qb = [lane_roll(a, 1) for a in q]
        fb = flux(qb, lane_roll(v[2], 1), lane_roll(pressure, 1), 2)
        low = face(qb, fb, lane_roll(speed, 1), q, f, speed)
        rate = (
            jnp.abs(v[0]) + sound + (jnp.abs(v[1]) + sound) + (jnp.abs(v[2]) + sound) * refinement
        )
        scale = (0.5 * COURANT) / rate
        r = i - 1
        slot = lax.rem(r, 8)
        for c in range(COMPS):
            inner = jnp.where(lane == 0, 0.0, low[c])
            difference = inner - lane_roll(inner, nz - 1)
            value = (total[c] + refinement * difference) * scale
            res_ref[c, r] = value
            strip = jnp.where(lane < 96, lane_roll(value, 64), value)
            strip = lane_roll(strip, lax.rem(slot * 16 + (nz - 88), nz))
            place = up_ref.at[c * groups + r // 8]
            place[...] = jnp.where((lane >= slot * 16) & (lane < slot * 16 + 16), strip, place[...])
            at = 32 * (c % 4) + 2 * r
            ends = down_ref.at[COMPS * half + c // 4]
            moved = lane_roll(q[c], lax.rem(at + 1, nz))
            ends[...] = jnp.where((lane == at) | (lane == at + 1), moved, ends[...])
            planes = up_ref.at[COMPS * groups + c // 4]
            above = lane_roll(q[c], lax.rem(at + 32, nz))
            beneath = lane_roll(q[c], lax.rem(at + 98, nz))
            planes[...] = jnp.where(
                lane == at, above, jnp.where(lane == at + 1, beneath, planes[...])
            )
        return qn, vn, pn, sn, face_high

    q0, q1 = load(0), load(1)
    v0, p0, s0 = primitives(q0)
    v1, p1, s1 = primitives(q1)
    low = face(
        q0, flux(q0, v0[0], p0, 0), jnp.abs(v0[0]) + s0, q1, flux(q1, v1[0], p1, 0), jnp.abs(v1[0]) + s1
    )
    lax.fori_loop(1, n + 1, row, (q1, v1, p1, s1, low))
    for c in range(COMPS):
        a = res_ref[c, :half].reshape(half * ny, nz)
        b = res_ref[c, half:].reshape(half * ny, nz)
        packed = exact_dot(a, w_ref[0]) + exact_dot(b, w_ref[1])
        down_ref[c * half : (c + 1) * half] = packed.reshape(half, ny, nz)


def residuals(n, upper, first, second, weights):
    ny, nz = first.shape[2:]
    half, groups = n // 2, -(-n // 8)
    return pl.pallas_call(
        functools.partial(residual_kernel, n, upper),
        out_shape=(
            jax.ShapeDtypeStruct((COMPS, n, ny, nz), F32),
            jax.ShapeDtypeStruct((COMPS * half + 2, ny, nz), F32),
            jax.ShapeDtypeStruct((COMPS * groups + 2, ny, nz), F32),
        ),
        in_specs=[pl.BlockSpec(memory_space=pltpu.VMEM)] * 3,
        out_specs=(pl.BlockSpec(memory_space=pltpu.VMEM),) * 3,
        scratch_shapes=[pltpu.VMEM((COMPS, 2 * ROWS, ny, nz), F32)],
        name="residual_upper" if upper else "residual_lower",
    )(first, second, weights)


def end_faces(ends, planes, refinement):
    shape = ends[0].shape
    upper = lax.rem(lanes(shape), 2) == 0

    def parts(pack):
        return [pack[0]] + [lane_roll(pack[0], 128 - 32 * c) for c in (1, 2, 3)] + [pack[1]]

    q, g = parts(ends), parts(planes)
    v, pressure, sound = primitives(q)
    vg, pg, sg = primitives(g)
    f, fg = flux(q, v[2], pressure, 2), flux(g, vg[2], pg, 2)
    speed = jnp.maximum(jnp.abs(v[2]) + sound, jnp.abs(vg[2]) + sg)
    rate = jnp.abs(v[0]) + sound + (jnp.abs(v[1]) + sound) + (jnp.abs(v[2]) + sound) * refinement
    scale = (0.5 * COURANT) * refinement / rate
    out = []
    for c in range(COMPS):
        jump = speed * (q[c] - g[c])
        mean = f[c] + fg[c]
        out.append(jnp.where(upper, -(mean + jump), mean - jump) * scale)
    return out


def target_rows(n, offset, flags, res_ref, down_own, up_own, down_got, up_got, t_ref, mask):
    level, refinement, top = flags
    half, groups = n // 2, -(-n // 8)
    ny, nz = t_ref.shape[2:]
    lane = lanes((ny, nz))
    covered = (lane >= 32) & (lane < 96)
    replaced = covered & (jnp.full((ny, nz), top, jnp.int32) == 0)
    ends = [down_own[COMPS * half + k] for k in range(2)]
    planes = [up_own[COMPS * groups + k] for k in range(2)]
    ends_finer = [jnp.where(top == 1, ends[k], down_got[COMPS * half + k]) for k in range(2)]
    planes_coarser = [
        jnp.where(level == 0, ends[k], up_got[COMPS * groups + k]) for k in range(2)
    ]
    fix_own = end_faces(ends, planes_coarser, refinement)
    fix_finer = end_faces(ends_finer, planes, 2.0 * refinement)
    scale = mask * (1.0 / (1.0 + 6.0 * SMOOTHING))

    def one(r, c, average_own, average_got):
        moved = lane_roll(fix_own[c], 127 - 2 * r)
        own = res_ref[c, r] + jnp.where((lane == 0) | (lane == 127), moved, 0.0)
        at32 = lax.rem(32 + 127 - 2 * r, nz)
        at95 = 95 - 2 * r
        got = average_got + jnp.where(
            lane == 32,
            0.5 * lane_roll(fix_finer[c], at32),
            jnp.where(lane == 95, 0.5 * lane_roll(fix_finer[c], at95), 0.0),
        )
        t_ref[c, offset + r] = jnp.where(replaced, got, own) * scale
        inside = average_own + jnp.where(
            lane == 32,
            0.5 * lane_roll(fix_own[c], at32),
            jnp.where(lane == 95, 0.5 * lane_roll(fix_own[c], at95), 0.0),
        )
        strip = lane_roll(up_got[c * groups + r // 8], lax.rem(216 - 16 * lax.rem(r, 8), nz))
        strip = jnp.where(lane < 64, lane_roll(strip, 64), strip)
        t_ref[COMPS + c, offset + r] = jnp.where(covered, inside, strip) * scale

    def pair(r, carried):
        for c in range(COMPS):
            mine, got = down_own[c * half + r], down_got[c * half + r]
            one(r, c, mine, got)
            one(r + half, c, lane_roll(mine, 64), lane_roll(got, 64))
        return carried

    lax.fori_loop(0, half, pair, 0)


def sweep_kernel(
    u_ref, res0, down0, up0, got_down0, got_up0, res1, down1, up1, got_down1, got_up1, w_ref,
    out_ref, t_ref, a_ref, b_ref,
):
    level, block, refinement = axis_flags()
    top = (level == lax.axis_size("level") - 1).astype(jnp.int32)
    keep_low = (block > 0).astype(F32)
    keep_high = (block < lax.axis_size("block") - 1).astype(F32)
    ny, nz = t_ref.shape[2:]
    flags = (level, refinement, top)
    total = 2 * HALO + ROWS
    target_rows(LATE, 0, flags, res0, down0, up0, got_down0, got_up0, t_ref, 1.0)
    target_rows(EARLY, LATE, flags, res1, down1, up1, got_down1, got_up1, t_ref, 1.0)

    def clear(i, carried):
        t_ref[:, i] = t_ref[:, i] * keep_low
        t_ref[:, i + HALO + ROWS] = t_ref[:, i + HALO + ROWS] * keep_high
        return carried

    lax.fori_loop(0, HALO, clear, 0)
    half_shape = (2 * COMPS, ny // 2, nz)
    lane = lanes((1, 1, nz))
    sub = sublanes((1, ny // 2, 1))
    weight = SMOOTHING / (1.0 + 6.0 * SMOOTHING)

    def shifted(x):
        left = jnp.where(lane == 0, 0.0, lane_roll(x, 1))
        right = jnp.where(lane == nz - 1, 0.0, lane_roll(x, nz - 1))
        return left + right

    def sweep(source, dest, s):
        def row(i, carried):
            scale = weight * jnp.where(
                i < HALO, keep_low, jnp.where(i >= HALO + ROWS, keep_high, 1.0)
            )
            low, high = source[:, i, : ny // 2], source[:, i, ny // 2 :]
            low_up, high_up = pltpu.roll(low, 1, 1), pltpu.roll(high, 1, 1)
            low_dn, high_dn = pltpu.roll(low, ny // 2 - 1, 1), pltpu.roll(high, ny // 2 - 1, 1)
            n_low = jnp.where(sub == 0, 0.0, low_up) + jnp.where(sub == ny // 2 - 1, high_dn, low_dn)
            n_high = jnp.where(sub == 0, low_up, high_up) + jnp.where(sub == ny // 2 - 1, 0.0, high_dn)
            n_low = n_low + shifted(low) + (source[:, i - 1, : ny // 2] + source[:, i + 1, : ny // 2])
            n_high = n_high + shifted(high) + (source[:, i - 1, ny // 2 :] + source[:, i + 1, ny // 2 :])
            dest[:, i, : ny // 2] = t_ref[:, i, : ny // 2] + scale * n_low
            dest[:, i, ny // 2 :] = t_ref[:, i, ny // 2 :] + scale * n_high
            return carried

        lax.fori_loop(s - 1, total - s + 1, row, 0)

    buffers = (a_ref, b_ref)
    source = t_ref
    for s in range(2, SWEEPS + 1):
        dest = buffers[s % 2]
        sweep(source, dest, s)
        source = dest
    has_coarser = (level > 0).astype(F32)
    for c in range(COMPS):
        coarse = source[COMPS + c, HALO : HALO + ROWS].reshape(ROWS * ny, nz)
        lifted = exact_dot(coarse, w_ref[2]).reshape(ROWS, ny, nz)
        out_ref[c] = u_ref[c] + source[c, HALO : HALO + ROWS] + lifted * has_coarser


def matrices(nz):
    k = np.arange(nz)
    w = np.zeros((3, nz, nz), np.float32)
    w[0, k, nz // 4 + k // 2] = 0.5
    w[1, k, (3 * nz // 4 + k // 2) % nz] = 0.5
    w[2, nz // 4 + k // 2, k] = 1.0
    return jnp.asarray(w, jnp.bfloat16)


def shards(flow_state):
    fields = flow_state[0]
    ny, nz = fields.shape[2:]
    levels, blocks = lax.axis_size("level"), lax.axis_size("block")
    weights = matrices(nz)
    rise = [(i, i + 1) for i in range(blocks - 1)]
    fall = [(i + 1, i) for i in range(blocks - 1)]
    finer = [(i, i + 1) for i in range(levels - 1)]
    coarser = [(i + 1, i) for i in range(levels - 1)]
    below = lax.ppermute(fields, "block", rise)
    above = lax.ppermute(fields, "block", fall)
    res1, down1, up1 = residuals(EARLY, True, fields, above, weights)
    got_down1 = lax.ppermute(down1, "level", coarser)
    got_up1 = lax.ppermute(up1, "level", finer)
    below, res1 = lax.optimization_barrier((below, res1))
    res0, down0, up0 = residuals(LATE, False, below, fields, weights)
    got_down0 = lax.ppermute(down0, "level", coarser)
    got_up0 = lax.ppermute(up0, "level", finer)
    total = 2 * HALO + ROWS
    out = pl.pallas_call(
        sweep_kernel,
        out_shape=jax.ShapeDtypeStruct(fields.shape, F32),
        in_specs=[pl.BlockSpec(memory_space=pltpu.VMEM)] * 12,
        out_specs=pl.BlockSpec(memory_space=pltpu.VMEM),
        scratch_shapes=[pltpu.VMEM((2 * COMPS, total, ny, nz), F32)] * 3,
        name="sweeps",
    )(fields, res0, down0, up0, got_down0, got_up0, res1, down1, up1, got_down1, got_up1, weights)
    return out[None]


def solution(mesh):
    spec = P("level", None, "block", None, None)
    return jax.shard_map(shards, mesh=mesh, in_specs=(spec,), out_specs=spec, check_vma=False)
```

```python
import functools

import jax
import jax.numpy as jnp
import numpy as np
from jax import lax
from jax.experimental import pallas as pl
from jax.experimental.pallas import tpu as pltpu
from jax.sharding import PartitionSpec as P

SWEEPS = 8
GAMMA = 1.4
COURANT = 0.8
SMOOTHING = 2.0
COMPS = 5
ROWS = 8
HALO = SWEEPS - 1
LINE = 16
LATE = ROWS
EARLY = ROWS + HALO - 1
F32 = jnp.float32


def lanes(shape):
    return lax.broadcasted_iota(jnp.int32, shape, len(shape) - 1)


def sublanes(shape):
    return lax.broadcasted_iota(jnp.int32, shape, len(shape) - 2)


def lane_roll(x, shift):
    return pltpu.roll(x, shift, x.ndim - 1)


def exact_dot(x, w):
    high = x.astype(jnp.bfloat16)
    rest = x - high.astype(F32)
    mid = rest.astype(jnp.bfloat16)
    low = (rest - mid.astype(F32)).astype(jnp.bfloat16)
    dot = functools.partial(jnp.dot, preferred_element_type=F32)
    return dot(high, w) + dot(mid, w) + dot(low, w)


def primitives(q):
    inverse = 1.0 / q[0]
    v = [q[1] * inverse, q[2] * inverse, q[3] * inverse]
    pressure = (GAMMA - 1.0) * (q[4] - 0.5 * (q[1] * v[0] + q[2] * v[1] + q[3] * v[2]))
    sound = jnp.sqrt(GAMMA * pressure * inverse)
    return v, pressure, sound


def flux(q, normal, pressure, d):
    out = [q[1 + d], q[1] * normal, q[2] * normal, q[3] * normal, (q[4] + pressure) * normal]
    out[1 + d] = out[1 + d] + pressure
    return out


def face(q_left, f_left, s_left, q_right, f_right, s_right):
    speed = jnp.maximum(s_left, s_right)
    return [
        (f_left[c] + f_right[c]) - speed * (q_right[c] - q_left[c]) for c in range(COMPS)
    ]


def axis_flags():
    level = lax.axis_index("level")
    block = lax.axis_index("block")
    refinement = jnp.left_shift(jnp.int32(1), level).astype(F32)
    return level, block, refinement


def orientation():
    block = lax.axis_index("block")
    place = lax.rem(block, LINE)
    mirrored = (place == LINE - 1).astype(jnp.int32)
    far = jnp.maximum(mirrored, (place == 0).astype(jnp.int32))
    lowest = (block == 0).astype(jnp.int32)
    highest = (block == lax.axis_size("block") - 1).astype(jnp.int32)
    first_outside = jnp.where(mirrored == 1, lowest, highest)
    second_outside = jnp.where(mirrored == 1, highest, lowest)
    return mirrored, far, first_outside, second_outside


def oriented(mirrored, j):
    return jnp.where(mirrored == 1, ROWS - 1 - j, j)


def residual_kernel(n, own_ref, near_ref, other_ref, w_ref, *refs):
    level, block, refinement = axis_flags()
    mirrored, far, first_outside, second_outside = orientation()
    first = n == EARLY
    if first:
        res_ref, down_ref, up_ref, x_ref = refs
    else:
        earlier_ref, res_ref, down_ref, sent_ref, x_ref = refs
        up_ref = sent_ref.at[earlier_ref.shape[0] :]
        sent_ref[: earlier_ref.shape[0]] = earlier_ref[...]
    half, groups = n // 2, -(-n // 8)
    ny, nz = x_ref.shape[2:]
    other = mirrored if first else far
    outside = first_outside if first else second_outside
    sign = jnp.where(mirrored == 1, -1.0, 1.0).astype(F32)
    edge = own_ref[:, oriented(mirrored, ROWS - 1 if first else 0)]

    def fetch(j, carried):
        at = oriented(mirrored, j)
        halo = jnp.where(other == 1, other_ref[:, at], near_ref[:, at])
        halo = jnp.where(outside == 1, edge, halo)
        x_ref[:, j] = own_ref[:, at] if first else halo
        x_ref[:, ROWS + j] = halo if first else own_ref[:, at]
        return carried

    lax.fori_loop(0, ROWS, fetch, 0, unroll=4)
    lane, sub = lanes((ny, nz)), sublanes((ny, nz))
    down_ref[COMPS * half :] = jnp.zeros((2, ny, nz), F32)
    up_ref[...] = jnp.zeros(up_ref.shape, F32)

    def load(i):
        return [x_ref[c, i] for c in range(COMPS)]

    def along(q, v, pressure):
        normal = sign * v[0]
        return [
            sign * q[1], q[1] * normal + sign * pressure, q[2] * normal, q[3] * normal, (q[4] + pressure) * normal
        ]

    def row(i, carried):
        q, v, pressure, sound, face_low = carried
        qn = load(i + 1)
        vn, pn, sn = primitives(qn)
        face_high = face(q, along(q, v, pressure), jnp.abs(v[0]) + sound, qn, along(qn, vn, pn), jnp.abs(vn[0]) + sn)
        total = [face_low[c] - face_high[c] for c in range(COMPS)]
        f = flux(q, v[1], pressure, 1)
        speed = jnp.abs(v[1]) + sound

        def below(a):
            return jnp.where(sub == 0, a, pltpu.roll(a, 1, 0))

        qb = [below(a) for a in q]
        fb = flux(qb, below(v[1]), below(pressure), 1)
        low = face(qb, fb, below(speed), q, f, speed)
        for c in range(COMPS):
            high = jnp.where(sub == ny - 1, 2.0 * f[c], pltpu.roll(low[c], ny - 1, 0))
            total[c] = total[c] + (low[c] - high)
        f = flux(q, v[2], pressure, 2)
        speed = jnp.abs(v[2]) + sound
        qb = [lane_roll(a, 1) for a in q]
        fb = flux(qb, lane_roll(v[2], 1), lane_roll(pressure, 1), 2)
        low = face(qb, fb, lane_roll(speed, 1), q, f, speed)
        rate = (
            jnp.abs(v[0]) + sound + (jnp.abs(v[1]) + sound) + (jnp.abs(v[2]) + sound) * refinement
        )
        scale = (0.5 * COURANT) / rate
        r = i - 1
        slot = lax.rem(r, 8)
        for c in range(COMPS):
            inner = jnp.where(lane == 0, 0.0, low[c])
            difference = inner - lane_roll(inner, nz - 1)
            value = (total[c] + refinement * difference) * scale
            res_ref[c, r] = value
            strip = jnp.where(lane < 96, lane_roll(value, 64), value)
            strip = lane_roll(strip, lax.rem(slot * 16 + (nz - 88), nz))
            place = up_ref.at[c * groups + r // 8]
            place[...] = jnp.where((lane >= slot * 16) & (lane < slot * 16 + 16), strip, place[...])
            at = 32 * (c % 4) + 2 * r
            ends = down_ref.at[COMPS * half + c // 4]
            moved = lane_roll(q[c], lax.rem(at + 1, nz))
            ends[...] = jnp.where((lane == at) | (lane == at + 1), moved, ends[...])
            planes = up_ref.at[COMPS * groups + c // 4]
            above = lane_roll(q[c], lax.rem(at + 32, nz))
            beneath = lane_roll(q[c], lax.rem(at + 98, nz))
            planes[...] = jnp.where(
                lane == at, above, jnp.where(lane == at + 1, beneath, planes[...])
            )
        return qn, vn, pn, sn, face_high

    q0, q1 = load(0), load(1)
    v0, p0, s0 = primitives(q0)
    v1, p1, s1 = primitives(q1)
    low = face(q0, along(q0, v0, p0), jnp.abs(v0[0]) + s0, q1, along(q1, v1, p1), jnp.abs(v1[0]) + s1)
    lax.fori_loop(1, n + 1, row, (q1, v1, p1, s1, low), unroll=2)
    for c in range(COMPS):
        a = res_ref[c, :half].reshape(half * ny, nz)
        b = res_ref[c, half:].reshape(half * ny, nz)
        packed = exact_dot(a, w_ref[0]) + exact_dot(b, w_ref[1])
        down_ref[c * half : (c + 1) * half] = packed.reshape(half, ny, nz)


def residuals(n, own, near, other, weights, *earlier):
    ny, nz = own.shape[2:]
    half, groups = n // 2, -(-n // 8)
    sent = COMPS * groups + 2 + sum(a.shape[0] for a in earlier)
    return pl.pallas_call(
        functools.partial(residual_kernel, n),
        out_shape=(
            jax.ShapeDtypeStruct((COMPS, n, ny, nz), F32),
            jax.ShapeDtypeStruct((COMPS * half + 2, ny, nz), F32),
            jax.ShapeDtypeStruct((sent, ny, nz), F32),
        ),
        in_specs=[pl.BlockSpec(memory_space=pltpu.VMEM)] * (4 + len(earlier)),
        out_specs=(pl.BlockSpec(memory_space=pltpu.VMEM),) * 3,
        scratch_shapes=[pltpu.VMEM((COMPS, 2 * ROWS, ny, nz), F32)],
        compiler_params=pltpu.CompilerParams(vmem_limit_bytes=8 * 2**20),
        name="residual_first" if n == EARLY else "residual_second",
    )(own, near, other, weights, *earlier)


def end_faces(ends, planes, refinement):
    shape = ends[0].shape
    upper = lax.rem(lanes(shape), 2) == 0

    def parts(pack):
        return [pack[0]] + [lane_roll(pack[0], 128 - 32 * c) for c in (1, 2, 3)] + [pack[1]]

    q, g = parts(ends), parts(planes)
    v, pressure, sound = primitives(q)
    vg, pg, sg = primitives(g)
    f, fg = flux(q, v[2], pressure, 2), flux(g, vg[2], pg, 2)
    speed = jnp.maximum(jnp.abs(v[2]) + sound, jnp.abs(vg[2]) + sg)
    rate = jnp.abs(v[0]) + sound + (jnp.abs(v[1]) + sound) + (jnp.abs(v[2]) + sound) * refinement
    scale = (0.5 * COURANT) * refinement / rate
    out = []
    for c in range(COMPS):
        jump = speed * (q[c] - g[c])
        mean = f[c] + fg[c]
        out.append(jnp.where(upper, -(mean + jump), mean - jump) * scale)
    return out


def target_rows(n, offset, flags, res_ref, down_own, up_own, down_got, up_got, t_ref, mask):
    level, refinement, top = flags
    half, groups = n // 2, -(-n // 8)
    ny, nz = t_ref.shape[2:]
    lane = lanes((ny, nz))
    covered = (lane >= 32) & (lane < 96)
    replaced = covered & (jnp.full((ny, nz), top, jnp.int32) == 0)
    ends = [down_own[COMPS * half + k] for k in range(2)]
    planes = [up_own[COMPS * groups + k] for k in range(2)]
    ends_finer = [jnp.where(top == 1, ends[k], down_got[COMPS * half + k]) for k in range(2)]
    planes_coarser = [
        jnp.where(level == 0, ends[k], up_got[COMPS * groups + k]) for k in range(2)
    ]
    fix_own = end_faces(ends, planes_coarser, refinement)
    fix_finer = end_faces(ends_finer, planes, 2.0 * refinement)
    scale = mask * (1.0 / (1.0 + 6.0 * SMOOTHING))

    def one(r, c, average_own, average_got):
        moved = lane_roll(fix_own[c], 127 - 2 * r)
        own = res_ref[c, r] + jnp.where((lane == 0) | (lane == 127), moved, 0.0)
        at32 = lax.rem(32 + 127 - 2 * r, nz)
        at95 = 95 - 2 * r
        got = average_got + jnp.where(
            lane == 32,
            0.5 * lane_roll(fix_finer[c], at32),
            jnp.where(lane == 95, 0.5 * lane_roll(fix_finer[c], at95), 0.0),
        )
        t_ref[c, offset + r] = jnp.where(replaced, got, own) * scale
        inside = average_own + jnp.where(
            lane == 32,
            0.5 * lane_roll(fix_own[c], at32),
            jnp.where(lane == 95, 0.5 * lane_roll(fix_own[c], at95), 0.0),
        )
        strip = lane_roll(up_got[c * groups + r // 8], lax.rem(216 - 16 * lax.rem(r, 8), nz))
        strip = jnp.where(lane < 64, lane_roll(strip, 64), strip)
        t_ref[COMPS + c, offset + r] = jnp.where(covered, inside, strip) * scale

    def pair(r, carried):
        for c in range(COMPS):
            mine, got = down_own[c * half + r], down_got[c * half + r]
            one(r, c, mine, got)
            one(r + half, c, lane_roll(mine, 64), lane_roll(got, 64))
        return carried

    lax.fori_loop(0, half, pair, 0)


def sweep_kernel(
    u_ref, res0, down0, got_down0, res1, down1, got_down1, up, got_up, w_ref, out_ref, t_ref, a_ref, b_ref,
):
    level, block, refinement = axis_flags()
    top = (level == lax.axis_size("level") - 1).astype(jnp.int32)
    mirrored, _, first_outside, second_outside = orientation()
    keep_low = (second_outside == 0).astype(F32)
    keep_high = (first_outside == 0).astype(F32)
    ny, nz = t_ref.shape[2:]
    flags = (level, refinement, top)
    total = 2 * HALO + ROWS
    split = COMPS * -(-EARLY // 8) + 2
    target_rows(LATE, 0, flags, res0, down0, up.at[split:], got_down0, got_up.at[split:], t_ref, 1.0)
    target_rows(EARLY, LATE, flags, res1, down1, up, got_down1, got_up, t_ref, 1.0)

    def clear(i, carried):
        t_ref[:, i] = t_ref[:, i] * keep_low
        t_ref[:, i + HALO + ROWS] = t_ref[:, i + HALO + ROWS] * keep_high
        return carried

    lax.fori_loop(0, HALO, clear, 0)
    half_shape = (2 * COMPS, ny // 2, nz)
    lane = lanes((1, 1, nz))
    sub = sublanes((1, ny // 2, 1))
    weight = SMOOTHING / (1.0 + 6.0 * SMOOTHING)

    def shifted(x):
        left = jnp.where(lane == 0, 0.0, lane_roll(x, 1))
        right = jnp.where(lane == nz - 1, 0.0, lane_roll(x, nz - 1))
        return left + right

    def sweep(source, dest, s):
        def row(i, carried):
            scale = weight * jnp.where(
                i < HALO, keep_low, jnp.where(i >= HALO + ROWS, keep_high, 1.0)
            )
            low, high = source[:, i, : ny // 2], source[:, i, ny // 2 :]
            low_up, high_up = pltpu.roll(low, 1, 1), pltpu.roll(high, 1, 1)
            low_dn, high_dn = pltpu.roll(low, ny // 2 - 1, 1), pltpu.roll(high, ny // 2 - 1, 1)
            n_low = jnp.where(sub == 0, 0.0, low_up) + jnp.where(sub == ny // 2 - 1, high_dn, low_dn)
            n_high = jnp.where(sub == 0, low_up, high_up) + jnp.where(sub == ny // 2 - 1, 0.0, high_dn)
            n_low = n_low + shifted(low) + (source[:, i - 1, : ny // 2] + source[:, i + 1, : ny // 2])
            n_high = n_high + shifted(high) + (source[:, i - 1, ny // 2 :] + source[:, i + 1, ny // 2 :])
            dest[:, i, : ny // 2] = t_ref[:, i, : ny // 2] + scale * n_low
            dest[:, i, ny // 2 :] = t_ref[:, i, ny // 2 :] + scale * n_high
            return carried

        lax.fori_loop(s - 1, total - s + 1, row, 0, unroll=4)

    buffers = (a_ref, b_ref)
    source = t_ref
    for s in range(2, SWEEPS + 1):
        dest = buffers[s % 2]
        sweep(source, dest, s)
        source = dest
    has_coarser = (level > 0).astype(F32)
    for c in range(COMPS):
        coarse = source[COMPS + c, HALO : HALO + ROWS].reshape(ROWS * ny, nz)
        lifted = exact_dot(coarse, w_ref[2]).reshape(ROWS, ny, nz)
        added = source[c, HALO : HALO + ROWS] + lifted * has_coarser
        for j in range(ROWS):
            at = oriented(mirrored, j)
            out_ref[c, at] = u_ref[c, at] + added[j]


def matrices(nz):
    k = np.arange(nz)
    w = np.zeros((3, nz, nz), np.float32)
    w[0, k, nz // 4 + k // 2] = 0.5
    w[1, k, (3 * nz // 4 + k // 2) % nz] = 0.5
    w[2, nz // 4 + k // 2, k] = 1.0
    return jnp.asarray(w, jnp.bfloat16)


def shards(flow_state):
    fields = flow_state[0]
    ny, nz = fields.shape[2:]
    levels, blocks = lax.axis_size("level"), lax.axis_size("block")
    weights = matrices(nz)
    inner = [i for i in range(blocks - 1) if i % LINE != LINE - 1]
    ends = [i for i in range(blocks - 1) if i % LINE == LINE - 1]
    rise = [(i, i + 1) for i in inner]
    fall = [(i + 1, i) for i in inner]
    swap = [(i, i + 1) for i in ends] + [(i + 1, i) for i in ends]
    finer = [(i, i + 1) for i in range(levels - 1)]
    coarser = [(i + 1, i) for i in range(levels - 1)]
    below = lax.ppermute(fields, "block", rise)
    above = lax.ppermute(fields, "block", fall)
    beyond = lax.ppermute(fields, "block", swap)
    res1, down1, up1 = residuals(EARLY, fields, above, below, weights)
    got_down1 = lax.ppermute(down1, "level", coarser)
    beyond, res1 = lax.optimization_barrier((beyond, res1))
    res0, down0, up = residuals(LATE, fields, below, beyond, weights, up1)
    got_down0 = lax.ppermute(down0, "level", coarser)
    got_up = lax.ppermute(up, "level", finer)
    total = 2 * HALO + ROWS
    out = pl.pallas_call(
        sweep_kernel,
        out_shape=jax.ShapeDtypeStruct(fields.shape, F32),
        in_specs=[pl.BlockSpec(memory_space=pltpu.VMEM)] * 10,
        out_specs=pl.BlockSpec(memory_space=pltpu.VMEM),
        scratch_shapes=[pltpu.VMEM((2 * COMPS, total, ny, nz), F32)] * 3,
        compiler_params=pltpu.CompilerParams(vmem_limit_bytes=16 * 2**20),
        name="sweeps",
    )(fields, res0, down0, got_down0, res1, down1, got_down1, up, got_up, weights)
    return out[None]


def solution(mesh):
    spec = P("level", None, "block", None, None)
    return jax.shard_map(shards, mesh=mesh, in_specs=(spec,), out_specs=spec, check_vma=False)
```

```python
import functools

import jax
import jax.numpy as jnp
import numpy as np
from jax import lax
from jax.experimental import pallas as pl
from jax.experimental.pallas import tpu as pltpu
from jax.sharding import PartitionSpec as P

SWEEPS = 8
GAMMA = 1.4
COURANT = 0.8
SMOOTHING = 2.0
COMPS = 5
ROWS = 8
HALO = SWEEPS - 1
LINE = 16
LATE = ROWS
EARLY = ROWS + HALO - 1
F32 = jnp.float32
UNROLL = 4


def lanes(shape):
    return lax.broadcasted_iota(jnp.int32, shape, len(shape) - 1)


def sublanes(shape):
    return lax.broadcasted_iota(jnp.int32, shape, len(shape) - 2)


def lane_roll(x, shift):
    return pltpu.roll(x, shift, x.ndim - 1)


def split_dot(x, w):
    high = x.astype(jnp.bfloat16)
    low = (x - high.astype(F32)).astype(jnp.bfloat16)
    dot = functools.partial(jnp.dot, preferred_element_type=F32)
    return dot(high, w) + dot(low, w)


def primitives(q):
    inverse = 1.0 / q[0]
    v = [q[1] * inverse, q[2] * inverse, q[3] * inverse]
    pressure = (GAMMA - 1.0) * (q[4] - 0.5 * (q[1] * v[0] + q[2] * v[1] + q[3] * v[2]))
    sound = jnp.sqrt(GAMMA * pressure * inverse)
    return v, pressure, sound


def flux(q, normal, pressure, d):
    out = [q[1 + d], q[1] * normal, q[2] * normal, q[3] * normal, (q[4] + pressure) * normal]
    out[1 + d] = out[1 + d] + pressure
    return out


def face(q_left, f_left, s_left, q_right, f_right, s_right):
    speed = jnp.maximum(s_left, s_right)
    return [
        (f_left[c] + f_right[c]) - speed * (q_right[c] - q_left[c]) for c in range(COMPS)
    ]


def axis_flags():
    level = lax.axis_index("level")
    block = lax.axis_index("block")
    refinement = jnp.left_shift(jnp.int32(1), level).astype(F32)
    return level, block, refinement


def orientation():
    block = lax.axis_index("block")
    place = lax.rem(block, LINE)
    mirrored = (place == LINE - 1).astype(jnp.int32)
    far = jnp.maximum(mirrored, (place == 0).astype(jnp.int32))
    lowest = (block == 0).astype(jnp.int32)
    highest = (block == lax.axis_size("block") - 1).astype(jnp.int32)
    first_outside = jnp.where(mirrored == 1, lowest, highest)
    second_outside = jnp.where(mirrored == 1, highest, lowest)
    return mirrored, far, first_outside, second_outside


def oriented(mirrored, j):
    return jnp.where(mirrored == 1, ROWS - 1 - j, j)


def residual_kernel(n, own_ref, near_ref, other_ref, w_ref, *refs):
    level, block, refinement = axis_flags()
    mirrored, far, first_outside, second_outside = orientation()
    first = n == EARLY
    if first:
        res_ref, down_ref, up_ref, x_ref, pack_ref = refs
    else:
        earlier_ref, res_ref, down_ref, sent_ref, far_ref, near_chip_ref, x_ref, pack_ref = refs
        up_ref = sent_ref.at[earlier_ref.shape[0] :]
        sent_ref[: earlier_ref.shape[0]] = earlier_ref[...]
    half, groups = n // 2, -(-n // 8)
    ny, nz = x_ref.shape[2:]
    other = mirrored if first else far
    outside = first_outside if first else second_outside
    sign = jnp.where(mirrored == 1, -1.0, 1.0).astype(F32)
    edge = own_ref[:, oriented(mirrored, ROWS - 1 if first else 0)]

    def fetch(j, carried):
        at = oriented(mirrored, j)
        halo = jnp.where(other == 1, other_ref[:, at], near_ref[:, at])
        halo = jnp.where(outside == 1, edge, halo)
        x_ref[:, j] = own_ref[:, at] if first else halo
        x_ref[:, ROWS + j] = halo if first else own_ref[:, at]
        return carried

    lax.fori_loop(0, ROWS, fetch, 0, unroll=4)
    lane, sub = lanes((ny, nz)), sublanes((ny, nz))
    up_ref[: COMPS * groups] = jnp.zeros((COMPS * groups, ny, nz), F32)
    pack_ref[...] = jnp.zeros(pack_ref.shape, F32)

    def load(i):
        return [x_ref[c, i] for c in range(COMPS)]

    def along(q, v, pressure):
        normal = sign * v[0]
        return [
            sign * q[1], q[1] * normal + sign * pressure, q[2] * normal, q[3] * normal, (q[4] + pressure) * normal
        ]

    def row(i, carried):
        q, v, pressure, sound, face_low = carried
        qn = load(i + 1)
        vn, pn, sn = primitives(qn)
        face_high = face(q, along(q, v, pressure), jnp.abs(v[0]) + sound, qn, along(qn, vn, pn), jnp.abs(vn[0]) + sn)
        total = [face_low[c] - face_high[c] for c in range(COMPS)]
        f = flux(q, v[1], pressure, 1)
        speed = jnp.abs(v[1]) + sound

        def below(a):
            return jnp.where(sub == 0, a, pltpu.roll(a, 1, 0))

        qb = [below(a) for a in q]
        fb = flux(qb, below(v[1]), below(pressure), 1)
        low = face(qb, fb, below(speed), q, f, speed)
        for c in range(COMPS):
            high = jnp.where(sub == ny - 1, 2.0 * f[c], pltpu.roll(low[c], ny - 1, 0))
            total[c] = total[c] + (low[c] - high)
        f = flux(q, v[2], pressure, 2)
        speed = jnp.abs(v[2]) + sound
        qb = [lane_roll(a, 1) for a in q]
        fb = flux(qb, lane_roll(v[2], 1), lane_roll(pressure, 1), 2)
        low = face(qb, fb, lane_roll(speed, 1), q, f, speed)
        rate = (
            jnp.abs(v[0]) + sound + (jnp.abs(v[1]) + sound) + (jnp.abs(v[2]) + sound) * refinement
        )
        scale = (0.5 * COURANT) / rate
        r = i - 1
        slot = lax.rem(r, 8)
        in_slot = ((lane >= slot * 7) & (lane < slot * 7 + 7)) | ((lane >= slot * 7 + 71) & (lane < slot * 7 + 78))
        picked = (lane == lax.rem(2 * r + nz - 1, nz)) | (lane == 2 * r) | (lane == 2 * r + 31) | (lane == 2 * r + 96)
        for c in range(COMPS):
            inner = jnp.where(lane == 0, 0.0, low[c])
            difference = inner - lane_roll(inner, nz - 1)
            value = (total[c] + refinement * difference) * scale
            res_ref[c, r] = value
            strip = lane_roll(value, lax.rem(slot * 7 + (nz - 25), nz))
            place = up_ref.at[c * groups + r // 8]
            place[...] = jnp.where(in_slot, strip, place[...])
            pack_ref[c] = jnp.where(picked, lane_roll(q[c], 2 * r), pack_ref[c])
        return qn, vn, pn, sn, face_high

    q0, q1 = load(0), load(1)
    v0, p0, s0 = primitives(q0)
    v1, p1, s1 = primitives(q1)
    low = face(q0, along(q0, v0, p0), jnp.abs(v0[0]) + s0, q1, along(q1, v1, p1), jnp.abs(v1[0]) + s1)
    lax.fori_loop(1, n + 1, row, (q1, v1, p1, s1, low), unroll=UNROLL)
    odd = lax.rem(lane, 2) == 1
    ends, planes = [None, None], [None, None]
    for c in range(COMPS):
        pack = pack_ref[c]
        plane = jnp.where(odd, lane_roll(pack, 31), lane_roll(pack, 97))
        k, shift = c // 4, 32 * (c % 4)
        if shift == 0:
            ends[k], planes[k] = pack, plane
        else:
            here = (lane >= shift - 1) & (lane < shift + 31)
            ends[k] = jnp.where(here, lane_roll(pack, shift), ends[k])
            planes[k] = jnp.where(here, lane_roll(plane, shift), planes[k])
    for k in range(2):
        down_ref[COMPS * half + k] = ends[k]
        up_ref[COMPS * groups + k] = planes[k]
    for c in range(COMPS):
        a = res_ref[c, :half].reshape(half * ny, nz)
        b = res_ref[c, half:].reshape(half * ny, nz)
        packed = split_dot(a, w_ref[0]) + split_dot(b, w_ref[1])
        down_ref[c * half : (c + 1) * half] = packed.reshape(half, ny, nz)
    if not first:
        odd_level = lax.rem(level, 2) == 1
        to_odd = (far_ref, near_chip_ref)
        for is_odd in (True, False):
            up_to, down_to = to_odd if is_odd else to_odd[::-1]

            @pl.when(odd_level if is_odd else jnp.logical_not(odd_level))
            def _(up_to=up_to, down_to=down_to):
                up_to[: sent_ref.shape[0]] = sent_ref[...]
                up_to[sent_ref.shape[0] :] = jnp.zeros((up_to.shape[0] - sent_ref.shape[0], ny, nz), F32)
                down_to[...] = down_ref[...]


def residuals(n, own, near, other, weights, *earlier):
    ny, nz = own.shape[2:]
    half, groups = n // 2, -(-n // 8)
    down = COMPS * half + 2
    up = COMPS * groups + 2 + sum(a.shape[0] for a in earlier)
    tiles = [down, up] + ([max(down, up)] * 2 if earlier else [])
    return pl.pallas_call(
        functools.partial(residual_kernel, n),
        out_shape=(jax.ShapeDtypeStruct((COMPS, n, ny, nz), F32),)
        + tuple(jax.ShapeDtypeStruct((k, ny, nz), F32) for k in tiles),
        in_specs=[pl.BlockSpec(memory_space=pltpu.VMEM)] * (4 + len(earlier)),
        out_specs=(pl.BlockSpec(memory_space=pltpu.VMEM),) * (1 + len(tiles)),
        scratch_shapes=[pltpu.VMEM((COMPS, 2 * ROWS, ny, nz), F32), pltpu.VMEM((COMPS, ny, nz), F32)],
        compiler_params=pltpu.CompilerParams(vmem_limit_bytes=8 * 2**20),
        name="residual_second" if earlier else "residual_first",
    )(own, near, other, weights, *earlier)


def end_faces(ends, planes, refinement):
    shape = ends[0].shape
    upper = lax.rem(lanes(shape), 2) == 1

    def parts(pack):
        return [pack[0]] + [lane_roll(pack[0], 128 - 32 * c) for c in (1, 2, 3)] + [pack[1]]

    q, g = parts(ends), parts(planes)
    v, pressure, sound = primitives(q)
    vg, pg, sg = primitives(g)
    f, fg = flux(q, v[2], pressure, 2), flux(g, vg[2], pg, 2)
    speed = jnp.maximum(jnp.abs(v[2]) + sound, jnp.abs(vg[2]) + sg)
    rate = jnp.abs(v[0]) + sound + (jnp.abs(v[1]) + sound) + (jnp.abs(v[2]) + sound) * refinement
    scale = (0.5 * COURANT) * refinement / rate
    out = []
    for c in range(COMPS):
        jump = speed * (q[c] - g[c])
        mean = f[c] + fg[c]
        out.append(jnp.where(upper, -(mean + jump), mean - jump) * scale)
    return out


def end_terms(n, flags, down_own, up_own, down_got, up_got, own_ref, finer_ref):
    level, refinement, top = flags
    half, groups = n // 2, -(-n // 8)
    ends = [down_own[COMPS * half + k] for k in range(2)]
    planes = [up_own[COMPS * groups + k] for k in range(2)]
    ends_finer = [jnp.where(top == 1, ends[k], down_got[COMPS * half + k]) for k in range(2)]
    planes_coarser = [jnp.where(level == 0, ends[k], up_got[COMPS * groups + k]) for k in range(2)]
    lane = lanes(ends[0].shape)
    near = (lane < 30) | (lane == lane.shape[-1] - 1)

    def halves(a):
        return 0.5 * jnp.where(lane < 64, lane_roll(a, 32), lane_roll(a, 96))

    for c, a in enumerate(end_faces(ends, planes_coarser, refinement)):
        own_ref[c] = jnp.where(near, a, halves(a))
    for c, a in enumerate(end_faces(ends_finer, planes, 2.0 * refinement)):
        finer_ref[c] = halves(a)


def sweep_kernel(
    u_ref, res0, down0, res1, down1, up, got_down1, got_far, got_near_chip, w_ref,
    out_ref, got_down0, got_up, t_ref, own0, own1, finer0, finer1,
):
    level, block, refinement = axis_flags()
    top = (level == lax.axis_size("level") - 1).astype(jnp.int32)
    mirrored, _, first_outside, second_outside = orientation()
    keep_low = (second_outside == 0).astype(F32)
    keep_high = (first_outside == 0).astype(F32)
    ny, nz = t_ref.shape[2:]
    flags = (level, refinement, top)
    total = 2 * HALO + ROWS
    odd_level = lax.rem(level, 2) == 1

    @pl.when(odd_level)
    def _():
        got_down0[...] = got_far[: got_down0.shape[0]]
        got_up[...] = got_near_chip[: got_up.shape[0]]

    @pl.when(jnp.logical_not(odd_level))
    def _():
        got_down0[...] = got_near_chip[: got_down0.shape[0]]
        got_up[...] = got_far[: got_up.shape[0]]

    split = COMPS * -(-EARLY // 8) + 2
    late = (LATE, res0, down0, got_down0, got_up.at[split:], own0, finer0)
    early = (EARLY, res1, down1, got_down1, got_up, own1, finer1)
    end_terms(LATE, flags, down0, up.at[split:], got_down0, got_up.at[split:], own0, finer0)
    end_terms(EARLY, flags, down1, up, got_down1, got_up, own1, finer1)

    lane = lanes((ny, nz))
    covered = (lane >= 32) & (lane < 96)
    replaced = covered & (jnp.full((ny, nz), top, jnp.int32) == 0)
    outer = (lane == 0) | (lane == nz - 1)
    brink = (lane == 32) | (lane == 95)
    share = 1.0 / (1.0 + 6.0 * SMOOTHING)
    h = ny // 2
    lane1, sub1 = lanes((h, nz)), sublanes((h, nz))
    weights = [SMOOTHING * share * k for k in (keep_low, 1.0, keep_high)]
    has_coarser = (level > 0).astype(F32)

    def zone(i):
        return 0 if i < HALO else 1 if i < HALO + ROWS else 2

    def sides(x):
        left = jnp.where(lane1 == 0, 0.0, lane_roll(x, 1))
        right = jnp.where(lane1 == nz - 1, 0.0, lane_roll(x, nz - 1))
        return left + right

    def smooth(which):
        def target(i):
            return t_ref[which, i, :h], t_ref[which, i, h:]

        rows = {i: target(i) for i in range(total)}
        for s in range(2, SWEEPS + 1):
            fresh = {}
            for i in range(s - 1, total - s + 1):
                low, high = rows[i]
                low_up, high_up = pltpu.roll(low, 1, 0), pltpu.roll(high, 1, 0)
                low_dn, high_dn = pltpu.roll(low, h - 1, 0), pltpu.roll(high, h - 1, 0)
                n_low = jnp.where(sub1 == 0, 0.0, low_up) + jnp.where(sub1 == h - 1, high_dn, low_dn)
                n_high = jnp.where(sub1 == 0, low_up, high_up) + jnp.where(sub1 == h - 1, 0.0, high_dn)
                n_low = (n_low + sides(low)) + (rows[i - 1][0] + rows[i + 1][0])
                n_high = (n_high + sides(high)) + (rows[i - 1][1] + rows[i + 1][1])
                t_low, t_high = target(i)
                w = weights[zone(i)]
                fresh[i] = (t_low + w * n_low, t_high + w * n_high)
            rows = fresh
        return [jnp.concatenate(rows[HALO + j], axis=0) for j in range(ROWS)]

    def component(c, carried):
        for n, res, down_own, down_got, up_got, own, finer in (late, early):
            half, groups = n // 2, -(-n // 8)
            offset = 0 if n == LATE else LATE
            own_c, finer_c = own[c], finer[c]
            for r in range(n):
                i = offset + r
                scale = share * (keep_low, 1.0, keep_high)[zone(i)]
                average = down_own[c * half + r % half]
                got = down_got[c * half + r % half]
                if r >= half:
                    average, got = lane_roll(average, 64), lane_roll(got, 64)
                back = (nz - 2 * r) % nz
                term = lane_roll(own_c, back) if back else own_c
                term_finer = lane_roll(finer_c, back) if back else finer_c
                mine = res[c, r] + jnp.where(outer, term, 0.0)
                got = got + jnp.where(brink, term_finer, 0.0)
                t_ref[0, i] = jnp.where(replaced, got, mine) * scale
                inside = average + jnp.where(brink, term, 0.0)
                shift = (25 - 7 * (r % 8)) % nz
                strip = lane_roll(up_got[c * groups + r // 8], shift)
                t_ref[1, i] = jnp.where(covered, inside, strip) * scale
        fine, coarse = smooth(0), smooth(1)
        lifted = split_dot(jnp.concatenate(coarse, axis=0), w_ref[2]).reshape(ROWS, ny, nz)
        for j in range(ROWS):
            at = oriented(mirrored, j)
            out_ref[c, at] = u_ref[c, at] + (fine[j] + lifted[j] * has_coarser)
        return carried

    lax.fori_loop(0, COMPS, component, 0)


def matrices(nz):
    k = np.arange(nz)
    w = np.zeros((3, nz, nz), np.float32)
    w[0, k, nz // 4 + k // 2] = 0.5
    w[1, k, (3 * nz // 4 + k // 2) % nz] = 0.5
    w[2, nz // 4 + k // 2, k] = 1.0
    return jnp.asarray(w, jnp.bfloat16)


def shards(flow_state):
    fields = flow_state[0]
    ny, nz = fields.shape[2:]
    levels, blocks = lax.axis_size("level"), lax.axis_size("block")
    weights = matrices(nz)
    inner = [i for i in range(blocks - 1) if i % LINE != LINE - 1]
    ends = [i for i in range(blocks - 1) if i % LINE == LINE - 1]
    rise = [(i, i + 1) for i in inner]
    fall = [(i + 1, i) for i in inner]
    swap = [(i, i + 1) for i in ends] + [(i + 1, i) for i in ends]
    finer = [(i, i + 1) for i in range(levels - 1)]
    coarser = [(i + 1, i) for i in range(levels - 1)]
    below = lax.ppermute(fields, "block", rise)
    above = lax.ppermute(fields, "block", fall)
    beyond = lax.ppermute(fields, "block", swap)
    res1, down1, up1 = residuals(EARLY, fields, above, below, weights)
    got_down1 = lax.ppermute(down1, "level", coarser)
    beyond, res1 = lax.optimization_barrier((beyond, res1))
    res0, down0, up, far, near_chip = residuals(LATE, fields, below, beyond, weights, up1)
    across = [(i, i + 1) for i in range(1, levels - 1, 2)] + [(i + 1, i) for i in range(1, levels - 1, 2)]
    within = [(i, i + 1) for i in range(0, levels - 1, 2)] + [(i + 1, i) for i in range(0, levels - 1, 2)]
    got_far = lax.ppermute(far, "level", across)
    got_near_chip = lax.ppermute(near_chip, "level", within)
    total = 2 * HALO + ROWS
    pair = pltpu.VMEM((COMPS, ny, nz), F32)
    out = pl.pallas_call(
        sweep_kernel,
        out_shape=jax.ShapeDtypeStruct(fields.shape, F32),
        in_specs=[pl.BlockSpec(memory_space=pltpu.VMEM)] * 10,
        out_specs=pl.BlockSpec(memory_space=pltpu.VMEM),
        scratch_shapes=[
            pltpu.VMEM(down0.shape, F32), pltpu.VMEM(up.shape, F32), pltpu.VMEM((2, total, ny, nz), F32),
            pair, pair, pair, pair,
        ],
        compiler_params=pltpu.CompilerParams(vmem_limit_bytes=16 * 2**20),
        name="sweeps",
    )(fields, res0, down0, res1, down1, up, got_down1, got_far, got_near_chip, weights)
    return out[None]


def solution(mesh):
    spec = P("level", None, "block", None, None)
    return jax.shard_map(shards, mesh=mesh, in_specs=(spec,), out_specs=spec, check_vma=False)
```

```python
import functools

import jax
import jax.numpy as jnp
import ml_dtypes
import numpy as np
from jax import lax
from jax.experimental import pallas as pl
from jax.experimental.pallas import tpu as pltpu
from jax.sharding import PartitionSpec as P

SWEEPS = 8
GAMMA = 1.4
COURANT = 0.8
SMOOTHING = 2.0
COMPS = 5
ROWS = 8
HALO = SWEEPS - 1
LINE = 16
LATE = ROWS
EARLY = ROWS + HALO - 1
F32 = jnp.float32
UNROLL = 4
FIRST_UP_TILES = 22


def lanes(shape):
    return lax.broadcasted_iota(jnp.int32, shape, len(shape) - 1)


def sublanes(shape):
    return lax.broadcasted_iota(jnp.int32, shape, len(shape) - 2)


def lane_roll(x, shift):
    return pltpu.roll(x, shift, x.ndim - 1)


def split_dot(x, w):
    high = x.astype(jnp.bfloat16)
    low = (x - high.astype(F32)).astype(jnp.bfloat16)
    dot = functools.partial(jnp.dot, preferred_element_type=F32)
    return dot(high, w) + dot(low, w)


def pairing(nz, base):
    k = lax.broadcasted_iota(jnp.int32, (nz, nz), 0)
    to = lax.broadcasted_iota(jnp.int32, (nz, nz), 1)
    return jnp.where(to == lax.rem(base + k // 2, nz), 0.5, 0.0).astype(jnp.bfloat16)


def transforms(nz):
    k = np.arange(1, nz + 1)
    sine = np.sqrt(2.0 / (nz + 1)) * np.sin(np.pi * np.outer(k, k) / (nz + 1))
    back = sine[:, nz // 4 + np.arange(nz) // 2]

    def parts(a):
        high = a.astype(ml_dtypes.bfloat16)
        low = (a - high.astype(np.float64)).astype(ml_dtypes.bfloat16)
        row = np.concatenate([high, low], axis=1)
        return np.concatenate([row, row], axis=0)

    factor = 2.0 * np.cos(np.pi * k / (nz + 1))
    return jnp.asarray(np.stack([parts(sine), parts(back)])), jnp.asarray(np.tile(factor, (8, 1)), F32)


def halved(x):
    high = x.astype(jnp.bfloat16)
    return jnp.concatenate([high, (x - high.astype(F32)).astype(jnp.bfloat16)], axis=1)


def transformed(parts, w):
    out = jnp.dot(parts, w, preferred_element_type=F32)
    nz = out.shape[1] // 2
    return out[:, :nz] + out[:, nz:]


def primitives(q):
    inverse = 1.0 / q[0]
    v = [q[1] * inverse, q[2] * inverse, q[3] * inverse]
    pressure = (GAMMA - 1.0) * (q[4] - 0.5 * (q[1] * v[0] + q[2] * v[1] + q[3] * v[2]))
    sound = jnp.sqrt(GAMMA * pressure * inverse)
    return v, pressure, sound


def flux(q, normal, pressure, d):
    out = [q[1 + d], q[1] * normal, q[2] * normal, q[3] * normal, (q[4] + pressure) * normal]
    out[1 + d] = out[1 + d] + pressure
    return out


def face(q_left, f_left, s_left, q_right, f_right, s_right):
    speed = jnp.maximum(s_left, s_right)
    return [
        (f_left[c] + f_right[c]) - speed * (q_right[c] - q_left[c]) for c in range(COMPS)
    ]


def axis_flags():
    level = lax.axis_index("level")
    block = lax.axis_index("block")
    refinement = jnp.left_shift(jnp.int32(1), level).astype(F32)
    return level, block, refinement


def orientation():
    block = lax.axis_index("block")
    place = lax.rem(block, LINE)
    mirrored = (place >= LINE - 2).astype(jnp.int32)
    source = jnp.where(place == LINE - 2, 2, jnp.where((place == 0) | (place == LINE - 1), 1, 0))
    lowest = (block == 0).astype(jnp.int32)
    highest = (block == lax.axis_size("block") - 1).astype(jnp.int32)
    first_outside = jnp.where(mirrored == 1, lowest, highest)
    second_outside = jnp.where(mirrored == 1, highest, lowest)
    return mirrored, source, first_outside, second_outside


def oriented(mirrored, j):
    return jnp.where(mirrored == 1, ROWS - 1 - j, j)


def residual_kernel(n, own_ref, *refs):
    level, block, refinement = axis_flags()
    mirrored, source, first_outside, second_outside = orientation()
    first = n == EARLY
    if first:
        *halos, res_ref, down_ref, up_ref, x_ref, pack_ref = refs
    else:
        *halos, res_ref, down_ref, up_ref, far_ref, near_chip_ref, x_ref, pack_ref = refs
    half, groups = n // 2, -(-n // 8)
    ny, nz = x_ref.shape[2:]
    choice = mirrored if first else source
    outside = first_outside if first else second_outside
    sign = jnp.where(mirrored == 1, -1.0, 1.0).astype(F32)
    up_ref[...] = jnp.zeros(up_ref.shape, F32)
    pack_ref[...] = jnp.zeros(pack_ref.shape, F32)
    edge = own_ref[:, oriented(mirrored, ROWS - 1 if first else 0)]

    def fetch(j, carried):
        at = oriented(mirrored, j)
        halo = halos[0][:, at]
        for k, ref in enumerate(halos[1:], 1):
            halo = jnp.where(choice == k, ref[:, at], halo)
        halo = jnp.where(outside == 1, edge, halo)
        x_ref[:, j] = own_ref[:, at] if first else halo
        x_ref[:, ROWS + j] = halo if first else own_ref[:, at]
        return carried

    lax.fori_loop(0, ROWS, fetch, 0, unroll=4)
    lane, sub = lanes((ny, nz)), sublanes((ny, nz))

    def load(i):
        return [x_ref[c, i] for c in range(COMPS)]

    def along(q, v, pressure):
        normal = sign * v[0]
        return [
            sign * q[1], q[1] * normal + sign * pressure, q[2] * normal, q[3] * normal, (q[4] + pressure) * normal
        ]

    def row(i, carried):
        q, v, pressure, sound, face_low = carried
        qn = load(i + 1)
        vn, pn, sn = primitives(qn)
        face_high = face(q, along(q, v, pressure), jnp.abs(v[0]) + sound, qn, along(qn, vn, pn), jnp.abs(vn[0]) + sn)
        total = [face_low[c] - face_high[c] for c in range(COMPS)]
        f = flux(q, v[1], pressure, 1)
        speed = jnp.abs(v[1]) + sound

        def below(a):
            return jnp.where(sub == 0, a, pltpu.roll(a, 1, 0))

        qb = [below(a) for a in q]
        fb = flux(qb, below(v[1]), below(pressure), 1)
        low = face(qb, fb, below(speed), q, f, speed)
        for c in range(COMPS):
            high = jnp.where(sub == ny - 1, 2.0 * f[c], pltpu.roll(low[c], ny - 1, 0))
            total[c] = total[c] + (low[c] - high)
        f = flux(q, v[2], pressure, 2)
        speed = jnp.abs(v[2]) + sound
        qb = [lane_roll(a, 1) for a in q]
        fb = flux(qb, lane_roll(v[2], 1), lane_roll(pressure, 1), 2)
        low = face(qb, fb, lane_roll(speed, 1), q, f, speed)
        rate = (
            jnp.abs(v[0]) + sound + (jnp.abs(v[1]) + sound) + (jnp.abs(v[2]) + sound) * refinement
        )
        scale = (0.5 * COURANT) / rate
        r = i - 1
        slot = lax.rem(r, 8)
        in_slot = ((lane >= slot * 7) & (lane < slot * 7 + 7)) | ((lane >= slot * 7 + 71) & (lane < slot * 7 + 78))
        picked = (lane == lax.rem(2 * r + nz - 1, nz)) | (lane == 2 * r) | (lane == 2 * r + 31) | (lane == 2 * r + 96)
        for c in range(COMPS):
            inner = jnp.where(lane == 0, 0.0, low[c])
            difference = inner - lane_roll(inner, nz - 1)
            value = (total[c] + refinement * difference) * scale
            res_ref[c, r] = value
            strip = lane_roll(value, lax.rem(slot * 7 + (nz - 25), nz))
            place = up_ref.at[c * groups + r // 8]
            place[...] = jnp.where(in_slot, strip, place[...])
            pack_ref[c] = jnp.where(picked, lane_roll(q[c], 2 * r), pack_ref[c])
        return qn, vn, pn, sn, face_high

    q0, q1 = load(0), load(1)
    v0, p0, s0 = primitives(q0)
    v1, p1, s1 = primitives(q1)
    low = face(q0, along(q0, v0, p0), jnp.abs(v0[0]) + s0, q1, along(q1, v1, p1), jnp.abs(v1[0]) + s1)
    lax.fori_loop(1, n + 1, row, (q1, v1, p1, s1, low), unroll=UNROLL)
    odd = lax.rem(lane, 2) == 1
    ends, planes = [None, None], [None, None]
    for c in range(COMPS):
        pack = pack_ref[c]
        plane = jnp.where(odd, lane_roll(pack, 31), lane_roll(pack, 97))
        k, shift = c // 4, 32 * (c % 4)
        if shift == 0:
            ends[k], planes[k] = pack, plane
        else:
            here = (lane >= shift - 1) & (lane < shift + 31)
            ends[k] = jnp.where(here, lane_roll(pack, shift), ends[k])
            planes[k] = jnp.where(here, lane_roll(plane, shift), planes[k])
    for k in range(2):
        down_ref[COMPS * half + k] = ends[k]
        up_ref[COMPS * groups + k] = planes[k]
    to_first, to_second = pairing(nz, nz // 4), pairing(nz, 3 * nz // 4)
    for c in range(COMPS):
        a = res_ref[c, :half].reshape(half * ny, nz)
        b = res_ref[c, half:].reshape(half * ny, nz)
        packed = split_dot(a, to_first) + split_dot(b, to_second)
        down_ref[c * half : (c + 1) * half] = packed.reshape(half, ny, nz)
    if not first:
        odd_level = lax.rem(level, 2) == 1
        to_odd = (far_ref, near_chip_ref)
        for is_odd in (True, False):
            up_to, down_to = to_odd if is_odd else to_odd[::-1]

            @pl.when(odd_level if is_odd else jnp.logical_not(odd_level))
            def _(up_to=up_to, down_to=down_to):
                up_to[: up_ref.shape[0]] = up_ref[...]
                up_to[up_ref.shape[0] :] = jnp.zeros((up_to.shape[0] - up_ref.shape[0], ny, nz), F32)
                down_to[...] = down_ref[...]


def residuals(n, own, *halos):
    ny, nz = own.shape[2:]
    first = n == EARLY
    half, groups = n // 2, -(-n // 8)
    down, up = COMPS * half + 2, COMPS * groups + 2
    tiles = (down, FIRST_UP_TILES) if first else (down, up, down, down)
    shapes = [(COMPS, n, ny, nz)] + [(k, ny, nz) for k in tiles]
    scratch = [pltpu.VMEM((COMPS, 2 * ROWS, ny, nz), F32), pltpu.VMEM((COMPS, ny, nz), F32)]
    vmem = pl.BlockSpec(memory_space=pltpu.VMEM)
    return pl.pallas_call(
        functools.partial(residual_kernel, n),
        out_shape=tuple(jax.ShapeDtypeStruct(k, F32) for k in shapes),
        in_specs=[vmem] * (1 + len(halos)),
        out_specs=(vmem,) * len(shapes),
        scratch_shapes=scratch,
        compiler_params=pltpu.CompilerParams(vmem_limit_bytes=8 * 2**20),
        cost_estimate=pl.CostEstimate(flops=2_000_000, bytes_accessed=2_000_000, transcendentals=0),
        name="residual_first" if first else "residual_second",
    )(own, *halos)


def end_faces(ends, planes, refinement):
    shape = ends[0].shape
    upper = lax.rem(lanes(shape), 2) == 1

    def parts(pack):
        return [pack[0]] + [lane_roll(pack[0], 128 - 32 * c) for c in (1, 2, 3)] + [pack[1]]

    q, g = parts(ends), parts(planes)
    v, pressure, sound = primitives(q)
    vg, pg, sg = primitives(g)
    f, fg = flux(q, v[2], pressure, 2), flux(g, vg[2], pg, 2)
    speed = jnp.maximum(jnp.abs(v[2]) + sound, jnp.abs(vg[2]) + sg)
    rate = jnp.abs(v[0]) + sound + (jnp.abs(v[1]) + sound) + (jnp.abs(v[2]) + sound) * refinement
    scale = (0.5 * COURANT) * refinement / rate
    out = []
    for c in range(COMPS):
        jump = speed * (q[c] - g[c])
        mean = f[c] + fg[c]
        out.append(jnp.where(upper, -(mean + jump), mean - jump) * scale)
    return out


def end_terms(n, flags, down_own, up_own, down_got, up_got, own_ref, finer_ref):
    level, refinement, top = flags
    half, groups = n // 2, -(-n // 8)
    ends = [down_own[COMPS * half + k] for k in range(2)]
    planes = [up_own[COMPS * groups + k] for k in range(2)]
    ends_finer = [jnp.where(top == 1, ends[k], down_got[COMPS * half + k]) for k in range(2)]
    planes_coarser = [jnp.where(level == 0, ends[k], up_got[COMPS * groups + k]) for k in range(2)]
    lane = lanes(ends[0].shape)
    near = (lane < 30) | (lane == lane.shape[-1] - 1)

    def halves(a):
        return 0.5 * jnp.where(lane < 64, lane_roll(a, 32), lane_roll(a, 96))

    for c, a in enumerate(end_faces(ends, planes_coarser, refinement)):
        own_ref[c] = jnp.where(near, a, halves(a))
    for c, a in enumerate(end_faces(ends_finer, planes, 2.0 * refinement)):
        finer_ref[c] = halves(a)


def sweep_kernel(
    n, w_ref, factor_ref, res, down_own, up_own, *refs
):
    first = n == EARLY
    if first:
        down_got, up_got, part_ref, t_ref, lhs_ref, own_ends, finer_ends = refs
    else:
        got_far, got_near_chip, u_ref, earlier_ref, out_ref, t_ref, lhs_ref, own_ends, finer_ends, down_got, up_got = refs
    level, block, refinement = axis_flags()
    top = (level == lax.axis_size("level") - 1).astype(jnp.int32)
    mirrored, _, first_outside, second_outside = orientation()
    keep_low = (second_outside == 0).astype(F32)
    keep_high = (first_outside == 0).astype(F32)
    ny, nz = t_ref.shape[2:]
    half, groups = n // 2, -(-n // 8)
    total = 2 * HALO + ROWS
    offset = LATE if first else 0
    if not first:
        odd_level = lax.rem(level, 2) == 1
        for is_odd in (True, False):
            down_from, up_from = (got_far, got_near_chip) if is_odd else (got_near_chip, got_far)

            @pl.when(odd_level if is_odd else jnp.logical_not(odd_level))
            def _(down_from=down_from, up_from=up_from):
                down_got[...] = down_from[...]
                up_got[...] = up_from[: up_got.shape[0]]

    end_terms(n, (level, refinement, top), down_own, up_own, down_got, up_got, own_ends, finer_ends)

    lane = lanes((ny, nz))
    covered = (lane >= 32) & (lane < 96)
    replaced = covered & (jnp.full((ny, nz), top, jnp.int32) == 0)
    outer = (lane == 0) | (lane == nz - 1)
    brink = (lane == 32) | (lane == 95)
    share = 1.0 / (1.0 + 6.0 * SMOOTHING)
    h = ny // 2
    sub1 = sublanes((h, nz))
    factor = factor_ref[...]
    weights = [SMOOTHING * share * k for k in (keep_low, 1.0, keep_high)]
    has_coarser = (level > 0).astype(F32)

    def zone(i):
        return 0 if i < HALO else 1 if i < HALO + ROWS else 2

    def add(terms):
        out = terms[0]
        for term in terms[1:]:
            out = out + term
        return out

    def smooth(which):
        def target(i):
            return t_ref[which, i, :h], t_ref[which, i, h:]

        rows = {offset + r: target(offset + r) for r in range(n)}
        for s in range(2, SWEEPS + 1):
            fresh = {}
            for i in range(s - 1, total - s + 1):
                if i in rows:
                    low, high = rows[i]
                    low_up, high_up = pltpu.roll(low, 1, 0), pltpu.roll(high, 1, 0)
                    low_dn, high_dn = pltpu.roll(low, h - 1, 0), pltpu.roll(high, h - 1, 0)
                    n_low = jnp.where(sub1 == 0, 0.0, low_up) + jnp.where(sub1 == h - 1, high_dn, low_dn)
                    n_high = jnp.where(sub1 == 0, low_up, high_up) + jnp.where(sub1 == h - 1, 0.0, high_dn)
                    around = [(n_low + factor * low, n_high + factor * high)]
                else:
                    around = []
                beside = [rows[k] for k in (i - 1, i + 1) if k in rows]
                if not around and not beside:
                    continue
                w = weights[zone(i)]
                new = [w * add([a[k] for a in around + beside]) for k in range(2)]
                if offset <= i < offset + n:
                    new = [a + b for a, b in zip(target(i), new)]
                fresh[i] = tuple(new)
            rows = fresh
        return [jnp.concatenate(rows[HALO + j], axis=0) for j in range(ROWS)]

    def component(c, carried):
        own_c, finer_c = own_ends[c], finer_ends[c]
        for r in range(n):
            i = offset + r
            scale = share * (keep_low, 1.0, keep_high)[zone(i)]
            average = down_own[c * half + r % half]
            got = down_got[c * half + r % half]
            if r >= half:
                average, got = lane_roll(average, 64), lane_roll(got, 64)
            back = (nz - 2 * r) % nz
            term = lane_roll(own_c, back) if back else own_c
            term_finer = lane_roll(finer_c, back) if back else finer_c
            mine = res[c, r] + jnp.where(outer, term, 0.0)
            got = got + jnp.where(brink, term_finer, 0.0)
            lhs_ref[r * ny : (r + 1) * ny] = halved(jnp.where(replaced, got, mine) * scale)
            inside = average + jnp.where(brink, term, 0.0)
            shift = (25 - 7 * (r % 8)) % nz
            strip = lane_roll(up_got[c * groups + r // 8], shift)
            lhs_ref[(n + r) * ny : (n + r + 1) * ny] = halved(jnp.where(covered, inside, strip) * scale)
        t_ref[:, offset : offset + n] = transformed(lhs_ref[...], w_ref[0]).reshape(2, n, ny, nz)
        fine, coarse = smooth(0), smooth(1)
        if first:
            for j in range(ROWS):
                part_ref[c, j] = fine[j]
                part_ref[COMPS + c, j] = coarse[j]
            return carried
        for j in range(ROWS):
            lhs_ref[j * ny : (j + 1) * ny] = halved(fine[j] + earlier_ref[c, j])
            lhs_ref[(ROWS + j) * ny : (ROWS + j + 1) * ny] = halved(coarse[j] + earlier_ref[COMPS + c, j])
        own = transformed(lhs_ref[: ROWS * ny], w_ref[0]).reshape(ROWS, ny, nz)
        lifted = transformed(lhs_ref[ROWS * ny : 2 * ROWS * ny], w_ref[1]).reshape(ROWS, ny, nz)
        for j in range(ROWS):
            at = oriented(mirrored, j)
            out_ref[c, at] = u_ref[c, at] + (own[j] + lifted[j] * has_coarser)
        return carried

    lax.fori_loop(0, COMPS, component, 0)


def sweeps(n, shape, *args):
    ny, nz = shape[2:]
    first = n == EARLY
    half, groups = n // 2, -(-n // 8)
    ends = pltpu.VMEM((COMPS, ny, nz), F32)
    out = (2 * COMPS, ROWS, ny, nz) if first else shape
    return pl.pallas_call(
        functools.partial(sweep_kernel, n),
        out_shape=jax.ShapeDtypeStruct(out, F32),
        in_specs=[pl.BlockSpec(memory_space=pltpu.VMEM)] * (2 + len(args)),
        out_specs=pl.BlockSpec(memory_space=pltpu.VMEM),
        scratch_shapes=[
            pltpu.VMEM((2, 2 * HALO + ROWS, ny, nz), F32), pltpu.VMEM((2 * n * ny, 2 * nz), jnp.bfloat16), ends, ends
        ]
        + ([] if first else [pltpu.VMEM((k, ny, nz), F32) for k in (COMPS * half + 2, COMPS * groups + 2)]),
        compiler_params=pltpu.CompilerParams(vmem_limit_bytes=16 * 2**20),
        cost_estimate=pl.CostEstimate(flops=10_000_000, bytes_accessed=10_000_000, transcendentals=0),
        name="sweeps_first" if first else "sweeps_second",
    )(*transforms(nz), *args)


def staged(x):
    def kernel(x_ref, out_ref):
        out_ref[...] = x_ref[...]

    vmem = pl.BlockSpec(memory_space=pltpu.VMEM)
    return pl.pallas_call(
        kernel,
        out_shape=jax.ShapeDtypeStruct(x.shape, F32),
        in_specs=[vmem],
        out_specs=vmem,
        compiler_params=pltpu.CompilerParams(vmem_limit_bytes=2 * 2**20),
        name="staged",
    )(x)


def shards(flow_state):
    fields = flow_state[0]
    ny, nz = fields.shape[2:]
    levels, blocks = lax.axis_size("level"), lax.axis_size("block")
    inner = [i for i in range(blocks - 1) if i % LINE != LINE - 1]
    ends = [i for i in range(blocks - 1) if i % LINE == LINE - 1]
    rise = [(i, i + 1) for i in inner]
    fall = [(i + 1, i) for i in inner if i % LINE != LINE - 2]
    last = [(i + 1, i) for i in inner if i % LINE == LINE - 2]
    swap = [(i, i + 1) for i in ends] + [(i + 1, i) for i in ends]
    finer = [(i, i + 1) for i in range(levels - 1)]
    coarser = [(i + 1, i) for i in range(levels - 1)]
    across = [(i, i + 1) for i in range(1, levels - 1, 2)] + [(i + 1, i) for i in range(1, levels - 1, 2)]
    within = [(i, i + 1) for i in range(0, levels - 1, 2)] + [(i + 1, i) for i in range(0, levels - 1, 2)]
    above = lax.ppermute(fields, "block", fall)
    below = lax.ppermute(fields, "block", rise)
    own = staged(fields)
    beyond = lax.ppermute(own, "block", swap)
    res1, down1, up1 = residuals(EARLY, own, above, below)
    got_down1 = lax.ppermute(down1, "level", coarser)
    got_up1 = lax.ppermute(up1, "level", finer)
    own, down1 = lax.optimization_barrier((own, down1))
    edge = lax.ppermute(own, "block", last)
    res0, down0, up0, far0, near0 = residuals(LATE, own, below, beyond, edge)
    got_far0 = lax.ppermute(far0, "level", across)
    got_near0 = lax.ppermute(near0, "level", within)
    res1, res0 = lax.optimization_barrier((res1, res0))
    part = sweeps(EARLY, fields.shape, res1, down1, up1, got_down1, got_up1)
    out = sweeps(LATE, fields.shape, res0, down0, up0, got_far0, got_near0, own, part)
    return out[None]


def solution(mesh):
    spec = P("level", None, "block", None, None)
    return jax.shard_map(shards, mesh=mesh, in_specs=(spec,), out_specs=spec, check_vma=False)
```

```python
import functools

import jax
import jax.numpy as jnp
import ml_dtypes
import numpy as np
from jax import lax
from jax.experimental import pallas as pl
from jax.experimental.pallas import tpu as pltpu
from jax.sharding import PartitionSpec as P

SWEEPS = 8
GAMMA = 1.4
COURANT = 0.8
SMOOTHING = 2.0
COMPS = 5
ROWS = 8
HALO = SWEEPS - 1
LINE = 16
LATE = ROWS
EARLY = ROWS + HALO - 1
F32 = jnp.float32
UNROLL = 4
FIRST_UP_TILES = 12


def lanes(shape):
    return lax.broadcasted_iota(jnp.int32, shape, len(shape) - 1)


def sublanes(shape):
    return lax.broadcasted_iota(jnp.int32, shape, len(shape) - 2)


def lane_roll(x, shift):
    return pltpu.roll(x, shift, x.ndim - 1)


def split_dot(x, w):
    high = x.astype(jnp.bfloat16)
    low = (x - high.astype(F32)).astype(jnp.bfloat16)
    dot = functools.partial(jnp.dot, preferred_element_type=F32)
    return dot(high, w) + dot(low, w)


def pairing(nz, base):
    k = lax.broadcasted_iota(jnp.int32, (nz, nz), 0)
    to = lax.broadcasted_iota(jnp.int32, (nz, nz), 1)
    return jnp.where(to == lax.rem(base + k // 2, nz), 0.5, 0.0).astype(jnp.bfloat16)


def transforms(nz):
    k = np.arange(1, nz + 1)
    sine = np.sqrt(2.0 / (nz + 1)) * np.sin(np.pi * np.outer(k, k) / (nz + 1))
    back = sine[:, nz // 4 + np.arange(nz) // 2]

    def parts(a):
        high = a.astype(ml_dtypes.bfloat16)
        low = (a - high.astype(np.float64)).astype(ml_dtypes.bfloat16)
        row = np.concatenate([high, low], axis=1)
        return np.concatenate([row, row], axis=0)

    return jnp.asarray(np.stack([parts(sine), parts(back)]))


def halved(x):
    high = x.astype(jnp.bfloat16)
    return jnp.concatenate([high, (x - high.astype(F32)).astype(jnp.bfloat16)], axis=1)


def transformed(parts, w):
    out = jnp.dot(parts, w, preferred_element_type=F32)
    nz = out.shape[1] // 2
    return out[:, :nz] + out[:, nz:]


def primitives(q):
    inverse = 1.0 / q[0]
    v = [q[1] * inverse, q[2] * inverse, q[3] * inverse]
    pressure = (GAMMA - 1.0) * (q[4] - 0.5 * (q[1] * v[0] + q[2] * v[1] + q[3] * v[2]))
    sound = jnp.sqrt(GAMMA * pressure * inverse)
    return v, pressure, sound


def flux(q, normal, pressure, d):
    out = [q[1 + d], q[1] * normal, q[2] * normal, q[3] * normal, (q[4] + pressure) * normal]
    out[1 + d] = out[1 + d] + pressure
    return out


def face(q_left, f_left, s_left, q_right, f_right, s_right):
    speed = jnp.maximum(s_left, s_right)
    return [
        (f_left[c] + f_right[c]) - speed * (q_right[c] - q_left[c]) for c in range(COMPS)
    ]


def axis_flags():
    level = lax.axis_index("level")
    block = lax.axis_index("block")
    refinement = jnp.left_shift(jnp.int32(1), level).astype(F32)
    return level, block, refinement


def orientation():
    block = lax.axis_index("block")
    place = lax.rem(block, LINE)
    mirrored = (place >= LINE - 2).astype(jnp.int32)
    source = jnp.where(place == LINE - 2, 2, jnp.where((place == 0) | (place == LINE - 1), 1, 0))
    lowest = (block == 0).astype(jnp.int32)
    highest = (block == lax.axis_size("block") - 1).astype(jnp.int32)
    first_outside = jnp.where(mirrored == 1, lowest, highest)
    second_outside = jnp.where(mirrored == 1, highest, lowest)
    return mirrored, source, first_outside, second_outside


def oriented(mirrored, j):
    return jnp.where(mirrored == 1, ROWS - 1 - j, j)


def residual_kernel(n, own_ref, *refs):
    level, block, refinement = axis_flags()
    mirrored, source, first_outside, second_outside = orientation()
    first = n == EARLY
    if first:
        *halos, res_ref, down_ref, up_ref, x_ref, pack_ref = refs
    else:
        *halos, res_ref, down_ref, up_ref, far_ref, near_chip_ref, x_ref, pack_ref = refs
    half, groups = n // 2, -(-n // 8)
    ny, nz = x_ref.shape[2:]
    choice = mirrored if first else source
    outside = first_outside if first else second_outside
    sign = jnp.where(mirrored == 1, -1.0, 1.0).astype(F32)
    up_ref[...] = jnp.zeros(up_ref.shape, F32)
    pack_ref[...] = jnp.zeros(pack_ref.shape, F32)
    edge = own_ref[:, oriented(mirrored, ROWS - 1 if first else 0)]

    def fetch(j, carried):
        at = oriented(mirrored, j)
        halo = halos[0][:, at]
        for k, ref in enumerate(halos[1:], 1):
            halo = jnp.where(choice == k, ref[:, at], halo)
        halo = jnp.where(outside == 1, edge, halo)
        x_ref[:, j] = own_ref[:, at] if first else halo
        x_ref[:, ROWS + j] = halo if first else own_ref[:, at]
        return carried

    lax.fori_loop(0, ROWS, fetch, 0, unroll=4)
    lane, sub = lanes((ny, nz)), sublanes((ny, nz))

    def load(i):
        return [x_ref[c, i] for c in range(COMPS)]

    def along(q, v, pressure):
        normal = sign * v[0]
        return [
            sign * q[1], q[1] * normal + sign * pressure, q[2] * normal, q[3] * normal, (q[4] + pressure) * normal
        ]

    def row(i, carried):
        q, v, pressure, sound, face_low = carried
        qn = load(i + 1)
        vn, pn, sn = primitives(qn)
        face_high = face(q, along(q, v, pressure), jnp.abs(v[0]) + sound, qn, along(qn, vn, pn), jnp.abs(vn[0]) + sn)
        total = [face_low[c] - face_high[c] for c in range(COMPS)]
        f = flux(q, v[1], pressure, 1)
        speed = jnp.abs(v[1]) + sound

        def below(a):
            return jnp.where(sub == 0, a, pltpu.roll(a, 1, 0))

        qb = [below(a) for a in q]
        fb = flux(qb, below(v[1]), below(pressure), 1)
        low = face(qb, fb, below(speed), q, f, speed)
        for c in range(COMPS):
            high = jnp.where(sub == ny - 1, 2.0 * f[c], pltpu.roll(low[c], ny - 1, 0))
            total[c] = total[c] + (low[c] - high)
        f = flux(q, v[2], pressure, 2)
        speed = jnp.abs(v[2]) + sound
        qb = [lane_roll(a, 1) for a in q]
        fb = flux(qb, lane_roll(v[2], 1), lane_roll(pressure, 1), 2)
        low = face(qb, fb, lane_roll(speed, 1), q, f, speed)
        rate = (
            jnp.abs(v[0]) + sound + (jnp.abs(v[1]) + sound) + (jnp.abs(v[2]) + sound) * refinement
        )
        scale = (0.5 * COURANT) / rate
        r = i - 1
        slot = lax.rem(r, 8)
        in_slot = ((lane >= slot * 7) & (lane < slot * 7 + 7)) | ((lane >= slot * 7 + 71) & (lane < slot * 7 + 78))
        picked = (lane == lax.rem(2 * r + nz - 1, nz)) | (lane == 2 * r) | (lane == 2 * r + 31) | (lane == 2 * r + 96)
        for c in range(COMPS):
            inner = jnp.where(lane == 0, 0.0, low[c])
            difference = inner - lane_roll(inner, nz - 1)
            value = (total[c] + refinement * difference) * scale
            res_ref[c, r] = value
            strip = lane_roll(value, lax.rem(slot * 7 + (nz - 25), nz))
            place = up_ref.at[c * groups + r // 8]
            place[...] = jnp.where(in_slot, strip, place[...])
            pack_ref[c] = jnp.where(picked, lane_roll(q[c], 2 * r), pack_ref[c])
        return qn, vn, pn, sn, face_high

    q0, q1 = load(0), load(1)
    v0, p0, s0 = primitives(q0)
    v1, p1, s1 = primitives(q1)
    low = face(q0, along(q0, v0, p0), jnp.abs(v0[0]) + s0, q1, along(q1, v1, p1), jnp.abs(v1[0]) + s1)
    lax.fori_loop(1, n + 1, row, (q1, v1, p1, s1, low), unroll=UNROLL)
    odd = lax.rem(lane, 2) == 1
    ends, planes = [None, None], [None, None]
    for c in range(COMPS):
        pack = pack_ref[c]
        plane = jnp.where(odd, lane_roll(pack, 31), lane_roll(pack, 97))
        k, shift = c // 4, 32 * (c % 4)
        if shift == 0:
            ends[k], planes[k] = pack, plane
        else:
            here = (lane >= shift - 1) & (lane < shift + 31)
            ends[k] = jnp.where(here, lane_roll(pack, shift), ends[k])
            planes[k] = jnp.where(here, lane_roll(plane, shift), planes[k])
    for k in range(2):
        down_ref[COMPS * half + k] = ends[k]
        up_ref[COMPS * groups + k] = planes[k]
    to_first, to_second = pairing(nz, nz // 4), pairing(nz, 3 * nz // 4)
    for c in range(COMPS):
        a = res_ref[c, :half].reshape(half * ny, nz)
        b = res_ref[c, half:].reshape(half * ny, nz)
        packed = split_dot(a, to_first) + split_dot(b, to_second)
        down_ref[c * half : (c + 1) * half] = packed.reshape(half, ny, nz)
    if not first:
        odd_level = lax.rem(level, 2) == 1
        to_odd = (far_ref, near_chip_ref)
        for is_odd in (True, False):
            up_to, down_to = to_odd if is_odd else to_odd[::-1]

            @pl.when(odd_level if is_odd else jnp.logical_not(odd_level))
            def _(up_to=up_to, down_to=down_to):
                up_to[: up_ref.shape[0]] = up_ref[...]
                up_to[up_ref.shape[0] :] = jnp.zeros((up_to.shape[0] - up_ref.shape[0], ny, nz), F32)
                down_to[...] = down_ref[...]


def residuals(n, own, *halos):
    ny, nz = own.shape[2:]
    first = n == EARLY
    half, groups = n // 2, -(-n // 8)
    down, up = COMPS * half + 2, COMPS * groups + 2
    tiles = (down, FIRST_UP_TILES) if first else (down, up, down, down)
    shapes = [(COMPS, n, ny, nz)] + [(k, ny, nz) for k in tiles]
    scratch = [pltpu.VMEM((COMPS, 2 * ROWS, ny, nz), F32), pltpu.VMEM((COMPS, ny, nz), F32)]
    vmem = pl.BlockSpec(memory_space=pltpu.VMEM)
    return pl.pallas_call(
        functools.partial(residual_kernel, n),
        out_shape=tuple(jax.ShapeDtypeStruct(k, F32) for k in shapes),
        in_specs=[vmem] * (1 + len(halos)),
        out_specs=(vmem,) * len(shapes),
        scratch_shapes=scratch,
        compiler_params=pltpu.CompilerParams(vmem_limit_bytes=8 * 2**20),
        cost_estimate=pl.CostEstimate(flops=2_000_000, bytes_accessed=2_000_000, transcendentals=0),
        name="residual_first" if first else "residual_second",
    )(own, *halos)


def end_faces(ends, planes, refinement):
    shape = ends[0].shape
    upper = lax.rem(lanes(shape), 2) == 1

    def parts(pack):
        return [pack[0]] + [lane_roll(pack[0], 128 - 32 * c) for c in (1, 2, 3)] + [pack[1]]

    q, g = parts(ends), parts(planes)
    v, pressure, sound = primitives(q)
    vg, pg, sg = primitives(g)
    f, fg = flux(q, v[2], pressure, 2), flux(g, vg[2], pg, 2)
    speed = jnp.maximum(jnp.abs(v[2]) + sound, jnp.abs(vg[2]) + sg)
    rate = jnp.abs(v[0]) + sound + (jnp.abs(v[1]) + sound) + (jnp.abs(v[2]) + sound) * refinement
    scale = (0.5 * COURANT) * refinement / rate
    out = []
    for c in range(COMPS):
        jump = speed * (q[c] - g[c])
        mean = f[c] + fg[c]
        out.append(jnp.where(upper, -(mean + jump), mean - jump) * scale)
    return out


def end_terms(n, flags, down_own, up_own, down_got, up_got, own_ref, finer_ref):
    level, refinement, top = flags
    half, groups = n // 2, -(-n // 8)
    ends = [down_own[COMPS * half + k] for k in range(2)]
    planes = [up_own[COMPS * groups + k] for k in range(2)]
    ends_finer = [jnp.where(top == 1, ends[k], down_got[COMPS * half + k]) for k in range(2)]
    planes_coarser = [jnp.where(level == 0, ends[k], up_got[COMPS * groups + k]) for k in range(2)]
    lane = lanes(ends[0].shape)
    near = (lane < 30) | (lane == lane.shape[-1] - 1)

    def halves(a):
        return 0.5 * jnp.where(lane < 64, lane_roll(a, 32), lane_roll(a, 96))

    for c, a in enumerate(end_faces(ends, planes_coarser, refinement)):
        own_ref[c] = jnp.where(near, a, halves(a))
    for c, a in enumerate(end_faces(ends_finer, planes, 2.0 * refinement)):
        finer_ref[c] = halves(a)


def sweep_kernel(
    n, w_ref, factor_ref, res, down_own, up_own, *refs
):
    first = n == EARLY
    if first:
        down_got, up_got, part_ref, t_ref, lhs_ref, own_ends, finer_ends = refs
    else:
        got_far, got_near_chip, u_ref, earlier_ref, out_ref, t_ref, lhs_ref, own_ends, finer_ends, down_got, up_got = refs
    level, block, refinement = axis_flags()
    top = (level == lax.axis_size("level") - 1).astype(jnp.int32)
    mirrored, _, first_outside, second_outside = orientation()
    keep_low = (second_outside == 0).astype(F32)
    keep_high = (first_outside == 0).astype(F32)
    ny, nz = t_ref.shape[2:]
    half, groups = n // 2, -(-n // 8)
    total = 2 * HALO + ROWS
    offset = LATE if first else 0
    if not first:
        odd_level = lax.rem(level, 2) == 1
        for is_odd in (True, False):
            down_from, up_from = (got_far, got_near_chip) if is_odd else (got_near_chip, got_far)

            @pl.when(odd_level if is_odd else jnp.logical_not(odd_level))
            def _(down_from=down_from, up_from=up_from):
                down_got[...] = down_from[...]
                up_got[...] = up_from[: up_got.shape[0]]

    end_terms(n, (level, refinement, top), down_own, up_own, down_got, up_got, own_ends, finer_ends)

    lane = lanes((ny, nz))
    covered = (lane >= 32) & (lane < 96)
    replaced = covered & (jnp.full((ny, nz), top, jnp.int32) == 0)
    outer = (lane == 0) | (lane == nz - 1)
    brink = (lane == 32) | (lane == 95)
    share = 1.0 / (1.0 + 6.0 * SMOOTHING)
    h = ny // 2
    sub1 = sublanes((h, nz))
    factor = factor_ref[...]
    weights = [SMOOTHING * share * k for k in (keep_low, 1.0, keep_high)]
    has_coarser = (level > 0).astype(F32)

    def zone(i):
        return 0 if i < HALO else 1 if i < HALO + ROWS else 2

    def add(terms):
        out = terms[0]
        for term in terms[1:]:
            out = out + term
        return out

    def smooth(which):
        def target(i):
            return t_ref[which, i, :h], t_ref[which, i, h:]

        rows = {offset + r: target(offset + r) for r in range(n)}
        for s in range(2, SWEEPS + 1):
            fresh = {}
            for i in range(s - 1, total - s + 1):
                if i in rows:
                    low, high = rows[i]
                    low_up, high_up = pltpu.roll(low, 1, 0), pltpu.roll(high, 1, 0)
                    low_dn, high_dn = pltpu.roll(low, h - 1, 0), pltpu.roll(high, h - 1, 0)
                    n_low = jnp.where(sub1 == 0, 0.0, low_up) + jnp.where(sub1 == h - 1, high_dn, low_dn)
                    n_high = jnp.where(sub1 == 0, low_up, high_up) + jnp.where(sub1 == h - 1, 0.0, high_dn)
                    around = [(n_low + factor * low, n_high + factor * high)]
                else:
                    around = []
                beside = [rows[k] for k in (i - 1, i + 1) if k in rows]
                if not around and not beside:
                    continue
                w = weights[zone(i)]
                new = [w * add([a[k] for a in around + beside]) for k in range(2)]
                if offset <= i < offset + n:
                    new = [a + b for a, b in zip(target(i), new)]
                fresh[i] = tuple(new)
            rows = fresh
        return [jnp.concatenate(rows[HALO + j], axis=0) for j in range(ROWS)]

    def component(c, carried):
        own_c, finer_c = own_ends[c], finer_ends[c]
        for r in range(n):
            i = offset + r
            scale = share * (keep_low, 1.0, keep_high)[zone(i)]
            average = down_own[c * half + r % half]
            got = down_got[c * half + r % half]
            if r >= half:
                average, got = lane_roll(average, 64), lane_roll(got, 64)
            back = (nz - 2 * r) % nz
            term = lane_roll(own_c, back) if back else own_c
            term_finer = lane_roll(finer_c, back) if back else finer_c
            mine = res[c, r] + jnp.where(outer, term, 0.0)
            got = got + jnp.where(brink, term_finer, 0.0)
            lhs_ref[r * ny : (r + 1) * ny] = halved(jnp.where(replaced, got, mine) * scale)
            inside = average + jnp.where(brink, term, 0.0)
            shift = (25 - 7 * (r % 8)) % nz
            strip = lane_roll(up_got[c * groups + r // 8], shift)
            lhs_ref[(n + r) * ny : (n + r + 1) * ny] = halved(jnp.where(covered, inside, strip) * scale)
        t_ref[:, offset : offset + n] = transformed(lhs_ref[...], w_ref[0]).reshape(2, n, ny, nz)
        fine, coarse = smooth(0), smooth(1)
        if first:
            for j in range(ROWS):
                part_ref[c, j] = fine[j]
                part_ref[COMPS + c, j] = coarse[j]
            return carried
        for j in range(ROWS):
            lhs_ref[j * ny : (j + 1) * ny] = halved(fine[j] + earlier_ref[c, j])
            lhs_ref[(ROWS + j) * ny : (ROWS + j + 1) * ny] = halved(coarse[j] + earlier_ref[COMPS + c, j])
        own = transformed(lhs_ref[: ROWS * ny], w_ref[0]).reshape(ROWS, ny, nz)
        lifted = transformed(lhs_ref[ROWS * ny : 2 * ROWS * ny], w_ref[1]).reshape(ROWS, ny, nz)
        for j in range(ROWS):
            at = oriented(mirrored, j)
            out_ref[c, at] = u_ref[c, at] + (own[j] + lifted[j] * has_coarser)
        return carried

    lax.fori_loop(0, COMPS, component, 0, unroll=COMPS)


def sweeps(n, shape, *args):
    ny, nz = shape[2:]
    first = n == EARLY
    half, groups = n // 2, -(-n // 8)
    ends = pltpu.VMEM((COMPS, ny, nz), F32)
    out = (2 * COMPS, ROWS, ny, nz) if first else shape
    return pl.pallas_call(
        functools.partial(sweep_kernel, n),
        out_shape=jax.ShapeDtypeStruct(out, F32),
        in_specs=[pl.BlockSpec(memory_space=pltpu.VMEM)] * (1 + len(args)),
        out_specs=pl.BlockSpec(memory_space=pltpu.VMEM),
        scratch_shapes=[
            pltpu.VMEM((2, 2 * HALO + ROWS, ny, nz), F32), pltpu.VMEM((2 * n * ny, 2 * nz), jnp.bfloat16), ends, ends
        ]
        + ([] if first else [pltpu.VMEM((k, ny, nz), F32) for k in (COMPS * half + 2, COMPS * groups + 2)]),
        compiler_params=pltpu.CompilerParams(vmem_limit_bytes=16 * 2**20),
        cost_estimate=pl.CostEstimate(flops=10000000000, bytes_accessed=100000000, transcendentals=0),
        name="sweeps_first" if first else "sweeps_second",
    )(transforms(nz), *args)


def factors(nz):
    def kernel(out_ref):
        out_ref[...] = 2.0 * jnp.cos((np.pi / (nz + 1)) * (lanes((8, nz)) + 1).astype(F32))

    return pl.pallas_call(
        kernel,
        out_shape=jax.ShapeDtypeStruct((8, nz), F32),
        out_specs=pl.BlockSpec(memory_space=pltpu.VMEM),
        compiler_params=pltpu.CompilerParams(vmem_limit_bytes=2 * 2**20),
        cost_estimate=pl.CostEstimate(flops=10000000000, bytes_accessed=100000000, transcendentals=0),
        name="factors",
    )()


def shards(flow_state):
    fields = flow_state[0]
    ny, nz = fields.shape[2:]
    levels, blocks = lax.axis_size("level"), lax.axis_size("block")
    inner = [i for i in range(blocks - 1) if i % LINE != LINE - 1]
    ends = [i for i in range(blocks - 1) if i % LINE == LINE - 1]
    rise = [(i, i + 1) for i in inner]
    fall = [(i + 1, i) for i in inner if i % LINE != LINE - 2]
    last = [(i + 1, i) for i in inner if i % LINE == LINE - 2]
    swap = [(i, i + 1) for i in ends] + [(i + 1, i) for i in ends]
    finer = [(i, i + 1) for i in range(levels - 1)]
    coarser = [(i + 1, i) for i in range(levels - 1)]
    across = [(i, i + 1) for i in range(1, levels - 1, 2)] + [(i + 1, i) for i in range(1, levels - 1, 2)]
    within = [(i, i + 1) for i in range(0, levels - 1, 2)] + [(i + 1, i) for i in range(0, levels - 1, 2)]
    above = lax.ppermute(fields, "block", fall)
    below = lax.ppermute(fields, "block", rise)
    sent, factor = lax.optimization_barrier((fields, factors(nz)))
    beyond = lax.ppermute(sent, "block", swap)
    res1, down1, up1 = residuals(EARLY, fields, above, below)
    got_down1 = lax.ppermute(down1, "level", coarser)
    got_up1 = lax.ppermute(up1, "level", finer)
    own, down1 = lax.optimization_barrier((fields, down1))
    edge = lax.ppermute(own, "block", last)
    res0, down0, up0, far0, near0 = residuals(LATE, own, below, beyond, edge)
    got_far0 = lax.ppermute(far0, "level", across)
    got_near0 = lax.ppermute(near0, "level", within)
    res1, res0 = lax.optimization_barrier((res1, res0))
    part = sweeps(EARLY, fields.shape, factor, res1, down1, up1, got_down1, got_up1)
    out = sweeps(LATE, fields.shape, factor, res0, down0, up0, got_far0, got_near0, own, part)
    return out[None]


def solution(mesh):
    spec = P("level", None, "block", None, None)
    return jax.shard_map(shards, mesh=mesh, in_specs=(spec,), out_specs=spec, check_vma=False)
```

```python
import functools

import jax
import jax.numpy as jnp
import ml_dtypes
import numpy as np
from jax import lax
from jax.experimental import pallas as pl
from jax.experimental.pallas import tpu as pltpu
from jax.sharding import PartitionSpec as P

SWEEPS = 8
GAMMA = 1.4
COURANT = 0.8
SMOOTHING = 2.0
COMPS = 5
ROWS = 8
HALO = SWEEPS - 1
LINE = 16
LATE = ROWS
EARLY = ROWS + HALO - 1
F32 = jnp.float32
UNROLL = 4
FIRST_UP_TILES = 12


def lanes(shape):
    return lax.broadcasted_iota(jnp.int32, shape, len(shape) - 1)


def sublanes(shape):
    return lax.broadcasted_iota(jnp.int32, shape, len(shape) - 2)


def lane_roll(x, shift):
    return pltpu.roll(x, shift, x.ndim - 1)


def split_dot(x, w):
    high = x.astype(jnp.bfloat16)
    low = (x - high.astype(F32)).astype(jnp.bfloat16)
    dot = functools.partial(jnp.dot, preferred_element_type=F32)
    return dot(high, w) + dot(low, w)


def pairing(nz, base):
    k = lax.broadcasted_iota(jnp.int32, (nz, nz), 0)
    to = lax.broadcasted_iota(jnp.int32, (nz, nz), 1)
    return jnp.where(to == lax.rem(base + k // 2, nz), 0.5, 0.0).astype(jnp.bfloat16)


def transforms(nz):
    k = np.arange(1, nz + 1)
    sine = np.sqrt(2.0 / (nz + 1)) * np.sin(np.pi * np.outer(k, k) / (nz + 1))
    back = sine[:, nz // 4 + np.arange(nz) // 2]

    def parts(a):
        high = a.astype(ml_dtypes.bfloat16)
        low = (a - high.astype(np.float64)).astype(ml_dtypes.bfloat16)
        row = np.concatenate([high, low], axis=1)
        return np.concatenate([row, row], axis=0)

    return jnp.asarray(np.stack([parts(sine), parts(back)]))


def halved(x):
    high = x.astype(jnp.bfloat16)
    return jnp.concatenate([high, (x - high.astype(F32)).astype(jnp.bfloat16)], axis=1)


def transformed(parts, w):
    out = jnp.dot(parts, w, preferred_element_type=F32)
    nz = out.shape[1] // 2
    return out[:, :nz] + out[:, nz:]


def primitives(q):
    inverse = 1.0 / q[0]
    v = [q[1] * inverse, q[2] * inverse, q[3] * inverse]
    pressure = (GAMMA - 1.0) * (q[4] - 0.5 * (q[1] * v[0] + q[2] * v[1] + q[3] * v[2]))
    sound = jnp.sqrt(GAMMA * pressure * inverse)
    return v, pressure, sound


def flux(q, normal, pressure, d):
    out = [q[1 + d], q[1] * normal, q[2] * normal, q[3] * normal, (q[4] + pressure) * normal]
    out[1 + d] = out[1 + d] + pressure
    return out


def face(q_left, f_left, s_left, q_right, f_right, s_right):
    speed = jnp.maximum(s_left, s_right)
    return [
        (f_left[c] + f_right[c]) - speed * (q_right[c] - q_left[c]) for c in range(COMPS)
    ]


def axis_flags():
    level = lax.axis_index("level")
    block = lax.axis_index("block")
    refinement = jnp.left_shift(jnp.int32(1), level).astype(F32)
    return level, block, refinement


def orientation():
    block = lax.axis_index("block")
    place = lax.rem(block, LINE)
    mirrored = (place >= LINE - 2).astype(jnp.int32)
    source = jnp.where(place == LINE - 2, 2, jnp.where((place == 0) | (place == LINE - 1), 1, 0))
    lowest = (block == 0).astype(jnp.int32)
    highest = (block == lax.axis_size("block") - 1).astype(jnp.int32)
    first_outside = jnp.where(mirrored == 1, lowest, highest)
    second_outside = jnp.where(mirrored == 1, highest, lowest)
    return mirrored, source, first_outside, second_outside


def oriented(mirrored, j):
    return jnp.where(mirrored == 1, ROWS - 1 - j, j)


def residual_kernel(n, own_ref, *refs):
    level, block, refinement = axis_flags()
    mirrored, source, first_outside, second_outside = orientation()
    first = n == EARLY
    if first:
        *halos, res_ref, down_ref, up_ref, x_ref, pack_ref = refs
    else:
        *halos, res_ref, down_ref, up_ref, far_ref, near_chip_ref, x_ref, pack_ref = refs
    half, groups = n // 2, -(-n // 8)
    ny, nz = x_ref.shape[2:]
    choice = mirrored if first else source
    outside = first_outside if first else second_outside
    sign = jnp.where(mirrored == 1, -1.0, 1.0).astype(F32)
    up_ref[...] = jnp.zeros(up_ref.shape, F32)
    pack_ref[...] = jnp.zeros(pack_ref.shape, F32)
    edge = own_ref[:, oriented(mirrored, ROWS - 1 if first else 0)]

    def fetch(j, carried):
        at = oriented(mirrored, j)
        halo = halos[0][:, at]
        for k, ref in enumerate(halos[1:], 1):
            halo = jnp.where(choice == k, ref[:, at], halo)
        halo = jnp.where(outside == 1, edge, halo)
        x_ref[:, j] = own_ref[:, at] if first else halo
        x_ref[:, ROWS + j] = halo if first else own_ref[:, at]
        return carried

    lax.fori_loop(0, ROWS, fetch, 0, unroll=4)
    lane, sub = lanes((ny, nz)), sublanes((ny, nz))

    def load(i):
        return [x_ref[c, i] for c in range(COMPS)]

    def along(q, v, pressure):
        normal = sign * v[0]
        return [
            sign * q[1], q[1] * normal + sign * pressure, q[2] * normal, q[3] * normal, (q[4] + pressure) * normal
        ]

    def row(i, carried):
        q, v, pressure, sound, face_low = carried
        qn = load(i + 1)
        vn, pn, sn = primitives(qn)
        face_high = face(q, along(q, v, pressure), jnp.abs(v[0]) + sound, qn, along(qn, vn, pn), jnp.abs(vn[0]) + sn)
        total = [face_low[c] - face_high[c] for c in range(COMPS)]
        f = flux(q, v[1], pressure, 1)
        speed = jnp.abs(v[1]) + sound

        def below(a):
            return jnp.where(sub == 0, a, pltpu.roll(a, 1, 0))

        qb = [below(a) for a in q]
        fb = flux(qb, below(v[1]), below(pressure), 1)
        low = face(qb, fb, below(speed), q, f, speed)
        for c in range(COMPS):
            high = jnp.where(sub == ny - 1, 2.0 * f[c], pltpu.roll(low[c], ny - 1, 0))
            total[c] = total[c] + (low[c] - high)
        f = flux(q, v[2], pressure, 2)
        speed = jnp.abs(v[2]) + sound
        qb = [lane_roll(a, 1) for a in q]
        fb = flux(qb, lane_roll(v[2], 1), lane_roll(pressure, 1), 2)
        low = face(qb, fb, lane_roll(speed, 1), q, f, speed)
        rate = (
            jnp.abs(v[0]) + sound + (jnp.abs(v[1]) + sound) + (jnp.abs(v[2]) + sound) * refinement
        )
        scale = (0.5 * COURANT) / rate
        r = i - 1
        slot = lax.rem(r, 8)
        in_slot = ((lane >= slot * 7) & (lane < slot * 7 + 7)) | ((lane >= slot * 7 + 71) & (lane < slot * 7 + 78))
        picked = (lane == lax.rem(2 * r + nz - 1, nz)) | (lane == 2 * r) | (lane == 2 * r + 31) | (lane == 2 * r + 96)
        for c in range(COMPS):
            inner = jnp.where(lane == 0, 0.0, low[c])
            difference = inner - lane_roll(inner, nz - 1)
            value = (total[c] + refinement * difference) * scale
            res_ref[c, r] = value
            strip = lane_roll(value, lax.rem(slot * 7 + (nz - 25), nz))
            place = up_ref.at[c * groups + r // 8]
            place[...] = jnp.where(in_slot, strip, place[...])
            pack_ref[c] = jnp.where(picked, lane_roll(q[c], 2 * r), pack_ref[c])
        return qn, vn, pn, sn, face_high

    q0, q1 = load(0), load(1)
    v0, p0, s0 = primitives(q0)
    v1, p1, s1 = primitives(q1)
    low = face(q0, along(q0, v0, p0), jnp.abs(v0[0]) + s0, q1, along(q1, v1, p1), jnp.abs(v1[0]) + s1)
    lax.fori_loop(1, n + 1, row, (q1, v1, p1, s1, low), unroll=UNROLL)
    odd = lax.rem(lane, 2) == 1
    ends, planes = [None, None], [None, None]
    for c in range(COMPS):
        pack = pack_ref[c]
        plane = jnp.where(odd, lane_roll(pack, 31), lane_roll(pack, 97))
        k, shift = c // 4, 32 * (c % 4)
        if shift == 0:
            ends[k], planes[k] = pack, plane
        else:
            here = (lane >= shift - 1) & (lane < shift + 31)
            ends[k] = jnp.where(here, lane_roll(pack, shift), ends[k])
            planes[k] = jnp.where(here, lane_roll(plane, shift), planes[k])
    for k in range(2):
        down_ref[COMPS * half + k] = ends[k]
        up_ref[COMPS * groups + k] = planes[k]
    to_first, to_second = pairing(nz, nz // 4), pairing(nz, 3 * nz // 4)
    for c in range(COMPS):
        a = res_ref[c, :half].reshape(half * ny, nz)
        b = res_ref[c, half:].reshape(half * ny, nz)
        packed = split_dot(a, to_first) + split_dot(b, to_second)
        down_ref[c * half : (c + 1) * half] = packed.reshape(half, ny, nz)
    if not first:
        odd_level = lax.rem(level, 2) == 1
        to_odd = (far_ref, near_chip_ref)
        for is_odd in (True, False):
            up_to, down_to = to_odd if is_odd else to_odd[::-1]

            @pl.when(odd_level if is_odd else jnp.logical_not(odd_level))
            def _(up_to=up_to, down_to=down_to):
                up_to[: up_ref.shape[0]] = up_ref[...]
                up_to[up_ref.shape[0] :] = jnp.zeros((up_to.shape[0] - up_ref.shape[0], ny, nz), F32)
                down_to[...] = down_ref[...]


def residuals(n, own, *halos):
    ny, nz = own.shape[2:]
    first = n == EARLY
    half, groups = n // 2, -(-n // 8)
    down, up = COMPS * half + 2, COMPS * groups + 2
    tiles = (down, FIRST_UP_TILES) if first else (down, up, down, down)
    shapes = [(COMPS, n, ny, nz)] + [(k, ny, nz) for k in tiles]
    scratch = [pltpu.VMEM((COMPS, 2 * ROWS, ny, nz), F32), pltpu.VMEM((COMPS, ny, nz), F32)]
    vmem = pl.BlockSpec(memory_space=pltpu.VMEM)
    return pl.pallas_call(
        functools.partial(residual_kernel, n),
        out_shape=tuple(jax.ShapeDtypeStruct(k, F32) for k in shapes),
        in_specs=[vmem] * (1 + len(halos)),
        out_specs=(vmem,) * len(shapes),
        scratch_shapes=scratch,
        compiler_params=pltpu.CompilerParams(vmem_limit_bytes=8 * 2**20),
        cost_estimate=pl.CostEstimate(flops=2_000_000, bytes_accessed=2_000_000, transcendentals=0),
        name="residual_first" if first else "residual_second",
    )(own, *halos)


def end_faces(ends, planes, refinement):
    shape = ends[0].shape
    upper = lax.rem(lanes(shape), 2) == 1

    def parts(pack):
        return [pack[0]] + [lane_roll(pack[0], 128 - 32 * c) for c in (1, 2, 3)] + [pack[1]]

    q, g = parts(ends), parts(planes)
    v, pressure, sound = primitives(q)
    vg, pg, sg = primitives(g)
    f, fg = flux(q, v[2], pressure, 2), flux(g, vg[2], pg, 2)
    speed = jnp.maximum(jnp.abs(v[2]) + sound, jnp.abs(vg[2]) + sg)
    rate = jnp.abs(v[0]) + sound + (jnp.abs(v[1]) + sound) + (jnp.abs(v[2]) + sound) * refinement
    scale = (0.5 * COURANT) * refinement / rate
    out = []
    for c in range(COMPS):
        jump = speed * (q[c] - g[c])
        mean = f[c] + fg[c]
        out.append(jnp.where(upper, -(mean + jump), mean - jump) * scale)
    return out


def end_terms(n, flags, down_own, up_own, down_got, up_got, own_ref, finer_ref):
    level, refinement, top = flags
    half, groups = n // 2, -(-n // 8)
    ends = [down_own[COMPS * half + k] for k in range(2)]
    planes = [up_own[COMPS * groups + k] for k in range(2)]
    ends_finer = [jnp.where(top == 1, ends[k], down_got[COMPS * half + k]) for k in range(2)]
    planes_coarser = [jnp.where(level == 0, ends[k], up_got[COMPS * groups + k]) for k in range(2)]
    lane = lanes(ends[0].shape)
    near = (lane < 30) | (lane == lane.shape[-1] - 1)

    def halves(a):
        return 0.5 * jnp.where(lane < 64, lane_roll(a, 32), lane_roll(a, 96))

    for c, a in enumerate(end_faces(ends, planes_coarser, refinement)):
        own_ref[c] = jnp.where(near, a, halves(a))
    for c, a in enumerate(end_faces(ends_finer, planes, 2.0 * refinement)):
        finer_ref[c] = halves(a)


def sweep_kernel(
    n, w_ref, factor_ref, res, down_own, up_own, *refs
):
    first = n == EARLY
    if first:
        down_got, up_got, part_ref, t_ref, lhs_ref, own_ends, finer_ends = refs
    else:
        got_far, got_near_chip, u_ref, earlier_ref, out_ref, t_ref, lhs_ref, own_ends, finer_ends, down_got, up_got = refs
    level, block, refinement = axis_flags()
    top = (level == lax.axis_size("level") - 1).astype(jnp.int32)
    mirrored, _, first_outside, second_outside = orientation()
    keep_low = (second_outside == 0).astype(F32)
    keep_high = (first_outside == 0).astype(F32)
    ny, nz = t_ref.shape[2:]
    half, groups = n // 2, -(-n // 8)
    total = 2 * HALO + ROWS
    offset = LATE if first else 0
    if not first:
        odd_level = lax.rem(level, 2) == 1
        for is_odd in (True, False):
            down_from, up_from = (got_far, got_near_chip) if is_odd else (got_near_chip, got_far)

            @pl.when(odd_level if is_odd else jnp.logical_not(odd_level))
            def _(down_from=down_from, up_from=up_from):
                down_got[...] = down_from[...]
                up_got[...] = up_from[: up_got.shape[0]]

    end_terms(n, (level, refinement, top), down_own, up_own, down_got, up_got, own_ends, finer_ends)

    lane = lanes((ny, nz))
    covered = (lane >= 32) & (lane < 96)
    replaced = covered & (jnp.full((ny, nz), top, jnp.int32) == 0)
    outer = (lane == 0) | (lane == nz - 1)
    brink = (lane == 32) | (lane == 95)
    share = 1.0 / (1.0 + 6.0 * SMOOTHING)
    h = ny // 2
    sub1 = sublanes((h, nz))
    factor = factor_ref[...]
    weights = [SMOOTHING * share * k for k in (keep_low, 1.0, keep_high)]
    has_coarser = (level > 0).astype(F32)

    def zone(i):
        return 0 if i < HALO else 1 if i < HALO + ROWS else 2

    def add(terms):
        out = terms[0]
        for term in terms[1:]:
            out = out + term
        return out

    def smooth(which):
        def target(i):
            return tuple(t_ref[which, i, pl.ds(k, h, stride=2)] for k in range(2))

        rows = {offset + r: target(offset + r) for r in range(n)}
        for s in range(2, SWEEPS + 1):
            fresh = {}
            for i in range(s - 1, total - s + 1):
                if i in rows:
                    even, odd = rows[i]
                    n_even = odd + jnp.where(sub1 == 0, 0.0, pltpu.roll(odd, 1, 0))
                    n_odd = even + jnp.where(sub1 == h - 1, 0.0, pltpu.roll(even, h - 1, 0))
                    around = [(n_even + factor * even, n_odd + factor * odd)]
                else:
                    around = []
                beside = [rows[k] for k in (i - 1, i + 1) if k in rows]
                if not around and not beside:
                    continue
                w = weights[zone(i)]
                new = [w * add([a[k] for a in around + beside]) for k in range(2)]
                if offset <= i < offset + n:
                    new = [a + b for a, b in zip(target(i), new)]
                fresh[i] = tuple(new)
            rows = fresh
        return [rows[HALO + j] for j in range(ROWS)]

    def component(c, carried):
        own_c, finer_c = own_ends[c], finer_ends[c]
        for r in range(n):
            i = offset + r
            scale = share * (keep_low, 1.0, keep_high)[zone(i)]
            average = down_own[c * half + r % half]
            got = down_got[c * half + r % half]
            if r >= half:
                average, got = lane_roll(average, 64), lane_roll(got, 64)
            back = (nz - 2 * r) % nz
            term = lane_roll(own_c, back) if back else own_c
            term_finer = lane_roll(finer_c, back) if back else finer_c
            mine = res[c, r] + jnp.where(outer, term, 0.0)
            got = got + jnp.where(brink, term_finer, 0.0)
            lhs_ref[r * ny : (r + 1) * ny] = halved(jnp.where(replaced, got, mine) * scale)
            inside = average + jnp.where(brink, term, 0.0)
            shift = (25 - 7 * (r % 8)) % nz
            strip = lane_roll(up_got[c * groups + r // 8], shift)
            lhs_ref[(n + r) * ny : (n + r + 1) * ny] = halved(jnp.where(covered, inside, strip) * scale)
        t_ref[:, offset : offset + n] = transformed(lhs_ref[...], w_ref[0]).reshape(2, n, ny, nz)
        fine, coarse = smooth(0), smooth(1)
        if first:
            for j in range(ROWS):
                for k in range(2):
                    part_ref[c, j, k * h : (k + 1) * h] = fine[j][k]
                    part_ref[COMPS + c, j, k * h : (k + 1) * h] = coarse[j][k]
            return carried
        for which, swept in enumerate((fine, coarse)):
            for j in range(ROWS):
                for k in range(2):
                    before = earlier_ref[which * COMPS + c, j, k * h : (k + 1) * h]
                    t_ref[which, j, pl.ds(k, h, stride=2)] = swept[j][k] + before
                at = which * ROWS + j
                lhs_ref[at * ny : (at + 1) * ny] = halved(t_ref[which, j])
        own = transformed(lhs_ref[: ROWS * ny], w_ref[0]).reshape(ROWS, ny, nz)
        lifted = transformed(lhs_ref[ROWS * ny : 2 * ROWS * ny], w_ref[1]).reshape(ROWS, ny, nz)
        for j in range(ROWS):
            at = oriented(mirrored, j)
            out_ref[c, at] = u_ref[c, at] + (own[j] + lifted[j] * has_coarser)
        return carried

    lax.fori_loop(0, COMPS, component, 0, unroll=COMPS)


def sweeps(n, shape, *args):
    ny, nz = shape[2:]
    first = n == EARLY
    half, groups = n // 2, -(-n // 8)
    ends = pltpu.VMEM((COMPS, ny, nz), F32)
    out = (2 * COMPS, ROWS, ny, nz) if first else shape
    return pl.pallas_call(
        functools.partial(sweep_kernel, n),
        out_shape=jax.ShapeDtypeStruct(out, F32),
        in_specs=[pl.BlockSpec(memory_space=pltpu.VMEM)] * (1 + len(args)),
        out_specs=pl.BlockSpec(memory_space=pltpu.VMEM),
        scratch_shapes=[
            pltpu.VMEM((2, 2 * HALO + ROWS, ny, nz), F32), pltpu.VMEM((2 * n * ny, 2 * nz), jnp.bfloat16), ends, ends
        ]
        + ([] if first else [pltpu.VMEM((k, ny, nz), F32) for k in (COMPS * half + 2, COMPS * groups + 2)]),
        compiler_params=pltpu.CompilerParams(vmem_limit_bytes=16 * 2**20),
        cost_estimate=pl.CostEstimate(flops=10000000000, bytes_accessed=100000000, transcendentals=0),
        name="sweeps_first" if first else "sweeps_second",
    )(transforms(nz), *args)


def factors(nz):
    def kernel(out_ref):
        out_ref[...] = 2.0 * jnp.cos((np.pi / (nz + 1)) * (lanes((8, nz)) + 1).astype(F32))

    return pl.pallas_call(
        kernel,
        out_shape=jax.ShapeDtypeStruct((8, nz), F32),
        out_specs=pl.BlockSpec(memory_space=pltpu.VMEM),
        compiler_params=pltpu.CompilerParams(vmem_limit_bytes=2 * 2**20),
        cost_estimate=pl.CostEstimate(flops=10000000000, bytes_accessed=100000000, transcendentals=0),
        name="factors",
    )()


def shards(flow_state):
    fields = flow_state[0]
    ny, nz = fields.shape[2:]
    levels, blocks = lax.axis_size("level"), lax.axis_size("block")
    inner = [i for i in range(blocks - 1) if i % LINE != LINE - 1]
    ends = [i for i in range(blocks - 1) if i % LINE == LINE - 1]
    rise = [(i, i + 1) for i in inner]
    fall = [(i + 1, i) for i in inner if i % LINE != LINE - 2]
    last = [(i + 1, i) for i in inner if i % LINE == LINE - 2]
    swap = [(i, i + 1) for i in ends] + [(i + 1, i) for i in ends]
    finer = [(i, i + 1) for i in range(levels - 1)]
    coarser = [(i + 1, i) for i in range(levels - 1)]
    across = [(i, i + 1) for i in range(1, levels - 1, 2)] + [(i + 1, i) for i in range(1, levels - 1, 2)]
    within = [(i, i + 1) for i in range(0, levels - 1, 2)] + [(i + 1, i) for i in range(0, levels - 1, 2)]
    above = lax.ppermute(fields, "block", fall)
    below = lax.ppermute(fields, "block", rise)
    sent, factor = lax.optimization_barrier((fields, factors(nz)))
    beyond = lax.ppermute(sent, "block", swap)
    res1, down1, up1 = residuals(EARLY, fields, above, below)
    got_down1 = lax.ppermute(down1, "level", coarser)
    got_up1 = lax.ppermute(up1, "level", finer)
    own, down1 = lax.optimization_barrier((fields, down1))
    edge = lax.ppermute(own, "block", last)
    res0, down0, up0, far0, near0 = residuals(LATE, own, below, beyond, edge)
    got_far0 = lax.ppermute(far0, "level", across)
    got_near0 = lax.ppermute(near0, "level", within)
    res1, res0 = lax.optimization_barrier((res1, res0))
    part = sweeps(EARLY, fields.shape, factor, res1, down1, up1, got_down1, got_up1)
    out = sweeps(LATE, fields.shape, factor, res0, down0, up0, got_far0, got_near0, own, part)
    return out[None]


def solution(mesh):
    spec = P("level", None, "block", None, None)
    return jax.shard_map(shards, mesh=mesh, in_specs=(spec,), out_specs=spec, check_vma=False)
```

```python
import functools

import jax
import jax.numpy as jnp
import ml_dtypes
import numpy as np
from jax import lax
from jax.experimental import pallas as pl
from jax.experimental.pallas import tpu as pltpu
from jax.sharding import PartitionSpec as P

SWEEPS = 8
GAMMA = 1.4
COURANT = 0.8
SMOOTHING = 2.0
COMPS = 5
ROWS = 8
HALO = SWEEPS - 1
LINE = 16
LATE = ROWS
EARLY = ROWS + HALO - 1
F32 = jnp.float32
UNROLL = 4
FIRST_UP_TILES = 12


def lanes(shape):
    return lax.broadcasted_iota(jnp.int32, shape, len(shape) - 1)


def sublanes(shape):
    return lax.broadcasted_iota(jnp.int32, shape, len(shape) - 2)


def lane_roll(x, shift):
    return pltpu.roll(x, shift, x.ndim - 1)


def split_dot(x, w):
    high = x.astype(jnp.bfloat16)
    low = (x - high.astype(F32)).astype(jnp.bfloat16)
    dot = functools.partial(jnp.dot, preferred_element_type=F32)
    return dot(high, w) + dot(low, w)


def pairing(nz, base):
    k = lax.broadcasted_iota(jnp.int32, (nz, nz), 0)
    to = lax.broadcasted_iota(jnp.int32, (nz, nz), 1)
    return jnp.where(to == lax.rem(base + k // 2, nz), 0.5, 0.0).astype(jnp.bfloat16)


def transforms(nz):
    k = np.arange(1, nz + 1)
    sine = np.sqrt(2.0 / (nz + 1)) * np.sin(np.pi * np.outer(k, k) / (nz + 1))
    back = sine[:, nz // 4 + np.arange(nz) // 2]

    def parts(a):
        high = a.astype(ml_dtypes.bfloat16)
        low = (a - high.astype(np.float64)).astype(ml_dtypes.bfloat16)
        row = np.concatenate([high, low], axis=1)
        return np.concatenate([row, row], axis=0)

    return jnp.asarray(np.stack([parts(sine), parts(back)]))


def halved(x):
    high = x.astype(jnp.bfloat16)
    return jnp.concatenate([high, (x - high.astype(F32)).astype(jnp.bfloat16)], axis=1)


def transformed(parts, w):
    out = jnp.dot(parts, w, preferred_element_type=F32)
    nz = out.shape[1] // 2
    return out[:, :nz] + out[:, nz:]


def primitives(q):
    inverse = 1.0 / q[0]
    v = [q[1] * inverse, q[2] * inverse, q[3] * inverse]
    pressure = (GAMMA - 1.0) * (q[4] - 0.5 * (q[1] * v[0] + q[2] * v[1] + q[3] * v[2]))
    sound = jnp.sqrt(GAMMA * pressure * inverse)
    return v, pressure, sound


def flux(q, normal, pressure, d):
    out = [q[1 + d], q[1] * normal, q[2] * normal, q[3] * normal, (q[4] + pressure) * normal]
    out[1 + d] = out[1 + d] + pressure
    return out


def face(q_left, f_left, s_left, q_right, f_right, s_right):
    speed = jnp.maximum(s_left, s_right)
    return [
        (f_left[c] + f_right[c]) - speed * (q_right[c] - q_left[c]) for c in range(COMPS)
    ]


def axis_flags():
    level = lax.axis_index("level")
    block = lax.axis_index("block")
    refinement = jnp.left_shift(jnp.int32(1), level).astype(F32)
    return level, block, refinement


def orientation():
    block = lax.axis_index("block")
    place = lax.rem(block, LINE)
    mirrored = (place >= LINE - 2).astype(jnp.int32)
    source = jnp.where(place == LINE - 2, 2, jnp.where((place == 0) | (place == LINE - 1), 1, 0))
    lowest = (block == 0).astype(jnp.int32)
    highest = (block == lax.axis_size("block") - 1).astype(jnp.int32)
    first_outside = jnp.where(mirrored == 1, lowest, highest)
    second_outside = jnp.where(mirrored == 1, highest, lowest)
    return mirrored, source, first_outside, second_outside


def oriented(mirrored, j):
    return jnp.where(mirrored == 1, ROWS - 1 - j, j)


def end_layout(n):
    width = 32 if n == EARLY else 16
    return width, 128 // width, -(-COMPS * width // 128)


def residual_kernel(n, own_ref, *refs):
    level, block, refinement = axis_flags()
    mirrored, source, first_outside, second_outside = orientation()
    first = n == EARLY
    if first:
        *halos, res_ref, down_ref, up_ref, x_ref, pack_ref = refs
    else:
        *halos, res_ref, down_ref, up_ref, far_ref, near_chip_ref, x_ref, pack_ref = refs
    half, groups = n // 2, -(-n // 8)
    ny, nz = x_ref.shape[2:]
    choice = mirrored if first else source
    outside = first_outside if first else second_outside
    sign = jnp.where(mirrored == 1, -1.0, 1.0).astype(F32)
    up_ref[...] = jnp.zeros(up_ref.shape, F32)
    pack_ref[...] = jnp.zeros(pack_ref.shape, F32)
    edge = own_ref[:, oriented(mirrored, ROWS - 1 if first else 0)]

    def fetch(j, carried):
        at = oriented(mirrored, j)
        halo = halos[0][:, at]
        for k, ref in enumerate(halos[1:], 1):
            halo = jnp.where(choice == k, ref[:, at], halo)
        halo = jnp.where(outside == 1, edge, halo)
        x_ref[:, j] = own_ref[:, at] if first else halo
        x_ref[:, ROWS + j] = halo if first else own_ref[:, at]
        return carried

    lax.fori_loop(0, ROWS, fetch, 0, unroll=4)
    lane, sub = lanes((ny, nz)), sublanes((ny, nz))

    def load(i):
        return [x_ref[c, i] for c in range(COMPS)]

    def along(q, v, pressure):
        normal = sign * v[0]
        return [
            sign * q[1], q[1] * normal + sign * pressure, q[2] * normal, q[3] * normal, (q[4] + pressure) * normal
        ]

    def row(i, carried):
        q, v, pressure, sound, face_low = carried
        qn = load(i + 1)
        vn, pn, sn = primitives(qn)
        face_high = face(q, along(q, v, pressure), jnp.abs(v[0]) + sound, qn, along(qn, vn, pn), jnp.abs(vn[0]) + sn)
        total = [face_low[c] - face_high[c] for c in range(COMPS)]
        f = flux(q, v[1], pressure, 1)
        speed = jnp.abs(v[1]) + sound

        def below(a):
            return jnp.where(sub == 0, a, pltpu.roll(a, 1, 0))

        qb = [below(a) for a in q]
        fb = flux(qb, below(v[1]), below(pressure), 1)
        low = face(qb, fb, below(speed), q, f, speed)
        for c in range(COMPS):
            high = jnp.where(sub == ny - 1, 2.0 * f[c], pltpu.roll(low[c], ny - 1, 0))
            total[c] = total[c] + (low[c] - high)
        f = flux(q, v[2], pressure, 2)
        speed = jnp.abs(v[2]) + sound
        qb = [lane_roll(a, 1) for a in q]
        fb = flux(qb, lane_roll(v[2], 1), lane_roll(pressure, 1), 2)
        low = face(qb, fb, lane_roll(speed, 1), q, f, speed)
        rate = (
            jnp.abs(v[0]) + sound + (jnp.abs(v[1]) + sound) + (jnp.abs(v[2]) + sound) * refinement
        )
        scale = (0.5 * COURANT) / rate
        r = i - 1
        slot = lax.rem(r, 8)
        in_slot = ((lane >= slot * 7) & (lane < slot * 7 + 7)) | ((lane >= slot * 7 + 71) & (lane < slot * 7 + 78))
        picked = (lane == lax.rem(2 * r + nz - 1, nz)) | (lane == 2 * r) | (lane == 2 * r + 31) | (lane == 2 * r + 96)
        for c in range(COMPS):
            inner = jnp.where(lane == 0, 0.0, low[c])
            difference = inner - lane_roll(inner, nz - 1)
            value = (total[c] + refinement * difference) * scale
            res_ref[c, r] = value
            strip = lane_roll(value, lax.rem(slot * 7 + (nz - 25), nz))
            place = up_ref.at[c * groups + r // 8]
            place[...] = jnp.where(in_slot, strip, place[...])
            pack_ref[c] = jnp.where(picked, lane_roll(q[c], 2 * r), pack_ref[c])
        return qn, vn, pn, sn, face_high

    q0, q1 = load(0), load(1)
    v0, p0, s0 = primitives(q0)
    v1, p1, s1 = primitives(q1)
    low = face(q0, along(q0, v0, p0), jnp.abs(v0[0]) + s0, q1, along(q1, v1, p1), jnp.abs(v1[0]) + s1)
    lax.fori_loop(1, n + 1, row, (q1, v1, p1, s1, low), unroll=UNROLL)
    odd = lax.rem(lane, 2) == 1
    width, each, tiles = end_layout(n)
    ends, planes = [None] * tiles, [None] * tiles
    for c in range(COMPS):
        pack = pack_ref[c]
        plane = jnp.where(odd, lane_roll(pack, 31), lane_roll(pack, 97))
        k, shift = c // each, width * (c % each)
        if shift == 0:
            ends[k], planes[k] = pack, plane
        else:
            here = (lane >= shift - 1) & (lane < shift + width - 1)
            ends[k] = jnp.where(here, lane_roll(pack, shift), ends[k])
            planes[k] = jnp.where(here, lane_roll(plane, shift), planes[k])
    for k in range(tiles):
        down_ref[COMPS * half + k] = ends[k]
        up_ref[COMPS * groups + k] = planes[k]
    to_first, to_second = pairing(nz, nz // 4), pairing(nz, 3 * nz // 4)
    for c in range(COMPS):
        a = res_ref[c, :half].reshape(half * ny, nz)
        b = res_ref[c, half:].reshape(half * ny, nz)
        packed = split_dot(a, to_first) + split_dot(b, to_second)
        down_ref[c * half : (c + 1) * half] = packed.reshape(half, ny, nz)
    if not first:
        odd_level = lax.rem(level, 2) == 1
        to_odd = (far_ref, near_chip_ref)
        for is_odd in (True, False):
            up_to, down_to = to_odd if is_odd else to_odd[::-1]

            @pl.when(odd_level if is_odd else jnp.logical_not(odd_level))
            def _(up_to=up_to, down_to=down_to):
                up_to[: up_ref.shape[0]] = up_ref[...]
                up_to[up_ref.shape[0] :] = jnp.zeros((up_to.shape[0] - up_ref.shape[0], ny, nz), F32)
                down_to[...] = down_ref[...]


def residuals(n, own, *halos):
    ny, nz = own.shape[2:]
    first = n == EARLY
    half, groups = n // 2, -(-n // 8)
    ends = end_layout(n)[2]
    down, up = COMPS * half + ends, COMPS * groups + ends
    tiles = (down, FIRST_UP_TILES) if first else (down, up, down, down)
    shapes = [(COMPS, n, ny, nz)] + [(k, ny, nz) for k in tiles]
    scratch = [pltpu.VMEM((COMPS, 2 * ROWS, ny, nz), F32), pltpu.VMEM((COMPS, ny, nz), F32)]
    vmem = pl.BlockSpec(memory_space=pltpu.VMEM)
    return pl.pallas_call(
        functools.partial(residual_kernel, n),
        out_shape=tuple(jax.ShapeDtypeStruct(k, F32) for k in shapes),
        in_specs=[vmem] * (1 + len(halos)),
        out_specs=(vmem,) * len(shapes),
        scratch_shapes=scratch,
        compiler_params=pltpu.CompilerParams(vmem_limit_bytes=8 * 2**20),
        cost_estimate=pl.CostEstimate(flops=2_000_000, bytes_accessed=2_000_000, transcendentals=0),
        name="residual_first" if first else "residual_second",
    )(own, *halos)


def end_faces(n, ends, planes, refinement):
    shape = ends[0].shape
    upper = lax.rem(lanes(shape), 2) == 1

    def parts(pack):
        width, each, _ = end_layout(n)
        return [lane_roll(pack[c // each], 128 - width * (c % each)) if c % each else pack[c // each] for c in range(COMPS)]

    q, g = parts(ends), parts(planes)
    v, pressure, sound = primitives(q)
    vg, pg, sg = primitives(g)
    f, fg = flux(q, v[2], pressure, 2), flux(g, vg[2], pg, 2)
    speed = jnp.maximum(jnp.abs(v[2]) + sound, jnp.abs(vg[2]) + sg)
    rate = jnp.abs(v[0]) + sound + (jnp.abs(v[1]) + sound) + (jnp.abs(v[2]) + sound) * refinement
    scale = (0.5 * COURANT) * refinement / rate
    out = []
    for c in range(COMPS):
        jump = speed * (q[c] - g[c])
        mean = f[c] + fg[c]
        out.append(jnp.where(upper, -(mean + jump), mean - jump) * scale)
    return out


def end_terms(n, flags, down_own, up_own, down_got, up_got, own_ref, finer_ref):
    level, refinement, top = flags
    tiles = end_layout(n)[2]
    half, groups = n // 2, -(-n // 8)
    ends = [down_own[COMPS * half + k] for k in range(tiles)]
    planes = [up_own[COMPS * groups + k] for k in range(tiles)]
    ends_finer = [jnp.where(top == 1, ends[k], down_got[COMPS * half + k]) for k in range(tiles)]
    planes_coarser = [jnp.where(level == 0, ends[k], up_got[COMPS * groups + k]) for k in range(tiles)]
    lane = lanes(ends[0].shape)
    near = (lane < 30) | (lane == lane.shape[-1] - 1)

    def halves(a):
        return 0.5 * jnp.where(lane < 64, lane_roll(a, 32), lane_roll(a, 96))

    for c, a in enumerate(end_faces(n, ends, planes_coarser, refinement)):
        own_ref[c] = jnp.where(near, a, halves(a))
    for c, a in enumerate(end_faces(n, ends_finer, planes, 2.0 * refinement)):
        finer_ref[c] = halves(a)


def sweep_kernel(
    n, w_ref, factor_ref, res, down_own, up_own, *refs
):
    first = n == EARLY
    if first:
        down_got, up_got, part_ref, t_ref, lhs_ref, own_ends, finer_ends = refs
    else:
        got_far, got_near_chip, u_ref, earlier_ref, out_ref, t_ref, lhs_ref, own_ends, finer_ends, down_got, up_got = refs
    level, block, refinement = axis_flags()
    top = (level == lax.axis_size("level") - 1).astype(jnp.int32)
    mirrored, _, first_outside, second_outside = orientation()
    keep_low = (second_outside == 0).astype(F32)
    keep_high = (first_outside == 0).astype(F32)
    ny, nz = t_ref.shape[2:]
    half, groups = n // 2, -(-n // 8)
    total = 2 * HALO + ROWS
    offset = LATE if first else 0
    if not first:
        odd_level = lax.rem(level, 2) == 1
        for is_odd in (True, False):
            down_from, up_from = (got_far, got_near_chip) if is_odd else (got_near_chip, got_far)

            @pl.when(odd_level if is_odd else jnp.logical_not(odd_level))
            def _(down_from=down_from, up_from=up_from):
                down_got[...] = down_from[...]
                up_got[...] = up_from[: up_got.shape[0]]

    end_terms(n, (level, refinement, top), down_own, up_own, down_got, up_got, own_ends, finer_ends)

    lane = lanes((ny, nz))
    covered = (lane >= 32) & (lane < 96)
    replaced = covered & (jnp.full((ny, nz), top, jnp.int32) == 0)
    outer = (lane == 0) | (lane == nz - 1)
    brink = (lane == 32) | (lane == 95)
    share = 1.0 / (1.0 + 6.0 * SMOOTHING)
    h = ny // 2
    sub1 = sublanes((h, nz))
    factor = factor_ref[...]
    weights = [SMOOTHING * share * k for k in (keep_low, 1.0, keep_high)]
    has_coarser = (level > 0).astype(F32)

    def zone(i):
        return 0 if i < HALO else 1 if i < HALO + ROWS else 2

    def add(terms):
        out = terms[0]
        for term in terms[1:]:
            out = out + term
        return out

    def smooth(which):
        def target(i):
            return tuple(t_ref[which, i, pl.ds(k, h, stride=2)] for k in range(2))

        rows = {offset + r: target(offset + r) for r in range(n)}
        for s in range(2, SWEEPS + 1):
            fresh = {}
            for i in range(s - 1, total - s + 1):
                if i in rows:
                    even, odd = rows[i]
                    n_even = odd + jnp.where(sub1 == 0, 0.0, pltpu.roll(odd, 1, 0))
                    n_odd = even + jnp.where(sub1 == h - 1, 0.0, pltpu.roll(even, h - 1, 0))
                    around = [(n_even + factor * even, n_odd + factor * odd)]
                else:
                    around = []
                beside = [rows[k] for k in (i - 1, i + 1) if k in rows]
                if not around and not beside:
                    continue
                w = weights[zone(i)]
                new = [w * add([a[k] for a in around + beside]) for k in range(2)]
                if offset <= i < offset + n:
                    new = [a + b for a, b in zip(target(i), new)]
                fresh[i] = tuple(new)
            rows = fresh
        return [rows[HALO + j] for j in range(ROWS)]

    def component(c, carried):
        own_c, finer_c = own_ends[c], finer_ends[c]
        for r in range(n):
            i = offset + r
            scale = share * (keep_low, 1.0, keep_high)[zone(i)]
            average = down_own[c * half + r % half]
            got = down_got[c * half + r % half]
            if r >= half:
                average, got = lane_roll(average, 64), lane_roll(got, 64)
            back = (nz - 2 * r) % nz
            term = lane_roll(own_c, back) if back else own_c
            term_finer = lane_roll(finer_c, back) if back else finer_c
            mine = res[c, r] + jnp.where(outer, term, 0.0)
            got = got + jnp.where(brink, term_finer, 0.0)
            lhs_ref[r * ny : (r + 1) * ny] = halved(jnp.where(replaced, got, mine) * scale)
            inside = average + jnp.where(brink, term, 0.0)
            shift = (25 - 7 * (r % 8)) % nz
            strip = lane_roll(up_got[c * groups + r // 8], shift)
            lhs_ref[(n + r) * ny : (n + r + 1) * ny] = halved(jnp.where(covered, inside, strip) * scale)
        t_ref[:, offset : offset + n] = transformed(lhs_ref[...], w_ref[0]).reshape(2, n, ny, nz)
        fine, coarse = smooth(0), smooth(1)
        if first:
            for j in range(ROWS):
                for k in range(2):
                    part_ref[c, j, k * h : (k + 1) * h] = fine[j][k]
                    part_ref[COMPS + c, j, k * h : (k + 1) * h] = coarse[j][k]
            return carried
        for which, swept in enumerate((fine, coarse)):
            for j in range(ROWS):
                for k in range(2):
                    before = earlier_ref[which * COMPS + c, j, k * h : (k + 1) * h]
                    t_ref[which, j, pl.ds(k, h, stride=2)] = swept[j][k] + before
                at = which * ROWS + j
                lhs_ref[at * ny : (at + 1) * ny] = halved(t_ref[which, j])
        own = transformed(lhs_ref[: ROWS * ny], w_ref[0]).reshape(ROWS, ny, nz)
        lifted = transformed(lhs_ref[ROWS * ny : 2 * ROWS * ny], w_ref[1]).reshape(ROWS, ny, nz)
        for j in range(ROWS):
            at = oriented(mirrored, j)
            out_ref[c, at] = u_ref[c, at] + (own[j] + lifted[j] * has_coarser)
        return carried

    lax.fori_loop(0, COMPS, component, 0, unroll=COMPS)


def sweeps(n, shape, *args):
    ny, nz = shape[2:]
    first = n == EARLY
    half, groups = n // 2, -(-n // 8)
    ends = pltpu.VMEM((COMPS, ny, nz), F32)
    out = (2 * COMPS, ROWS, ny, nz) if first else shape
    return pl.pallas_call(
        functools.partial(sweep_kernel, n),
        out_shape=jax.ShapeDtypeStruct(out, F32),
        in_specs=[pl.BlockSpec(memory_space=pltpu.VMEM)] * (1 + len(args)),
        out_specs=pl.BlockSpec(memory_space=pltpu.VMEM),
        scratch_shapes=[
            pltpu.VMEM((2, 2 * HALO + ROWS, ny, nz), F32), pltpu.VMEM((2 * n * ny, 2 * nz), jnp.bfloat16), ends, ends
        ]
        + ([] if first else [pltpu.VMEM((k, ny, nz), F32) for k in (COMPS * half + end_layout(n)[2], COMPS * groups + end_layout(n)[2])]),
        compiler_params=pltpu.CompilerParams(vmem_limit_bytes=16 * 2**20),
        cost_estimate=pl.CostEstimate(flops=10000000000, bytes_accessed=100000000, transcendentals=0),
        name="sweeps_first" if first else "sweeps_second",
    )(transforms(nz), *args)


def factors(nz):
    def kernel(out_ref):
        out_ref[...] = 2.0 * jnp.cos((np.pi / (nz + 1)) * (lanes((8, nz)) + 1).astype(F32))

    return pl.pallas_call(
        kernel,
        out_shape=jax.ShapeDtypeStruct((8, nz), F32),
        out_specs=pl.BlockSpec(memory_space=pltpu.VMEM),
        compiler_params=pltpu.CompilerParams(vmem_limit_bytes=2 * 2**20),
        cost_estimate=pl.CostEstimate(flops=10000000000, bytes_accessed=100000000, transcendentals=0),
        name="factors",
    )()


def shards(flow_state):
    fields = flow_state[0]
    ny, nz = fields.shape[2:]
    levels, blocks = lax.axis_size("level"), lax.axis_size("block")
    inner = [i for i in range(blocks - 1) if i % LINE != LINE - 1]
    ends = [i for i in range(blocks - 1) if i % LINE == LINE - 1]
    rise = [(i, i + 1) for i in inner]
    fall = [(i + 1, i) for i in inner if i % LINE != LINE - 2]
    last = [(i + 1, i) for i in inner if i % LINE == LINE - 2]
    swap = [(i, i + 1) for i in ends] + [(i + 1, i) for i in ends]
    finer = [(i, i + 1) for i in range(levels - 1)]
    coarser = [(i + 1, i) for i in range(levels - 1)]
    across = [(i, i + 1) for i in range(1, levels - 1, 2)] + [(i + 1, i) for i in range(1, levels - 1, 2)]
    within = [(i, i + 1) for i in range(0, levels - 1, 2)] + [(i + 1, i) for i in range(0, levels - 1, 2)]
    above = lax.ppermute(fields, "block", fall)
    below = lax.ppermute(fields, "block", rise)
    sent, factor = lax.optimization_barrier((fields, factors(nz)))
    beyond = lax.ppermute(sent, "block", swap)
    res1, down1, up1 = residuals(EARLY, fields, above, below)
    got_down1 = lax.ppermute(down1, "level", coarser)
    got_up1 = lax.ppermute(up1, "level", finer)
    own, down1 = lax.optimization_barrier((fields, down1))
    edge = lax.ppermute(own, "block", last)
    res0, down0, up0, far0, near0 = residuals(LATE, own, below, beyond, edge)
    got_far0 = lax.ppermute(far0, "level", across)
    got_near0 = lax.ppermute(near0, "level", within)
    res1, res0 = lax.optimization_barrier((res1, res0))
    part = sweeps(EARLY, fields.shape, factor, res1, down1, up1, got_down1, got_up1)
    out = sweeps(LATE, fields.shape, factor, res0, down0, up0, got_far0, got_near0, own, part)
    return out[None]


def solution(mesh):
    spec = P("level", None, "block", None, None)
    return jax.shard_map(shards, mesh=mesh, in_specs=(spec,), out_specs=spec, check_vma=False)
```

```python
import functools

import jax
import jax.numpy as jnp
import ml_dtypes
import numpy as np
from jax import lax
from jax.experimental import pallas as pl
from jax.experimental.pallas import tpu as pltpu
from jax.sharding import PartitionSpec as P

SWEEPS = 8
GAMMA = 1.4
COURANT = 0.8
SMOOTHING = 2.0
COMPS = 5
ROWS = 8
HALO = SWEEPS - 1
LINE = 16
LATE = ROWS
EARLY = ROWS + HALO - 1
F32 = jnp.float32
UNROLL = 4
FIRST_UP_TILES = 12


def lanes(shape):
    return lax.broadcasted_iota(jnp.int32, shape, len(shape) - 1)


def sublanes(shape):
    return lax.broadcasted_iota(jnp.int32, shape, len(shape) - 2)


def lane_roll(x, shift):
    return pltpu.roll(x, shift, x.ndim - 1)


def split_dot(x, w):
    high = x.astype(jnp.bfloat16)
    low = (x - high.astype(F32)).astype(jnp.bfloat16)
    dot = functools.partial(jnp.dot, preferred_element_type=F32)
    return dot(high, w) + dot(low, w)


def pairing(nz, base):
    k = lax.broadcasted_iota(jnp.int32, (nz, nz), 0)
    to = lax.broadcasted_iota(jnp.int32, (nz, nz), 1)
    return jnp.where(to == lax.rem(base + k // 2, nz), 0.5, 0.0).astype(jnp.bfloat16)


def transforms(nz):
    k = np.arange(1, nz + 1)
    sine = np.sqrt(2.0 / (nz + 1)) * np.sin(np.pi * np.outer(k, k) / (nz + 1))
    back = sine[:, nz // 4 + np.arange(nz) // 2]

    def parts(a):
        high = a.astype(ml_dtypes.bfloat16)
        low = (a - high.astype(np.float64)).astype(ml_dtypes.bfloat16)
        row = np.concatenate([high, low], axis=1)
        return np.concatenate([row, row], axis=0)

    return jnp.asarray(np.stack([parts(sine), parts(back)]))


def halved(x):
    high = x.astype(jnp.bfloat16)
    return jnp.concatenate([high, (x - high.astype(F32)).astype(jnp.bfloat16)], axis=1)


def transformed(parts, w):
    out = jnp.dot(parts, w, preferred_element_type=F32)
    nz = out.shape[1] // 2
    return out[:, :nz] + out[:, nz:]


def primitives(q):
    inverse = 1.0 / q[0]
    v = [q[1] * inverse, q[2] * inverse, q[3] * inverse]
    pressure = (GAMMA - 1.0) * (q[4] - 0.5 * (q[1] * v[0] + q[2] * v[1] + q[3] * v[2]))
    sound = jnp.sqrt(GAMMA * pressure * inverse)
    return v, pressure, sound


def flux(q, normal, pressure, d):
    out = [q[1 + d], q[1] * normal, q[2] * normal, q[3] * normal, (q[4] + pressure) * normal]
    out[1 + d] = out[1 + d] + pressure
    return out


def face(q_left, f_left, s_left, q_right, f_right, s_right):
    speed = jnp.maximum(s_left, s_right)
    return [
        (f_left[c] + f_right[c]) - speed * (q_right[c] - q_left[c]) for c in range(COMPS)
    ]


def axis_flags():
    level = lax.axis_index("level")
    block = lax.axis_index("block")
    refinement = jnp.left_shift(jnp.int32(1), level).astype(F32)
    return level, block, refinement


def orientation():
    block = lax.axis_index("block")
    place = lax.rem(block, LINE)
    mirrored = (place >= LINE - 2).astype(jnp.int32)
    source = jnp.where(place == LINE - 2, 2, jnp.where((place == 0) | (place == LINE - 1), 1, 0))
    lowest = (block == 0).astype(jnp.int32)
    highest = (block == lax.axis_size("block") - 1).astype(jnp.int32)
    first_outside = jnp.where(mirrored == 1, lowest, highest)
    second_outside = jnp.where(mirrored == 1, highest, lowest)
    return mirrored, source, first_outside, second_outside


def oriented(mirrored, j):
    return jnp.where(mirrored == 1, ROWS - 1 - j, j)


def end_layout(n):
    width = 32 if n == EARLY else 16
    return width, 128 // width, -(-COMPS * width // 128)


def residual_kernel(n, own_ref, *refs):
    level, block, refinement = axis_flags()
    mirrored, source, first_outside, second_outside = orientation()
    first = n == EARLY
    if first:
        *halos, res_ref, down_ref, up_ref, x_ref, pack_ref = refs
    else:
        *halos, res_ref, down_ref, up_ref, far_ref, near_chip_ref, x_ref, pack_ref = refs
    half, groups = n // 2, -(-n // 8)
    ny, nz = x_ref.shape[2:]
    choice = mirrored if first else source
    outside = first_outside if first else second_outside
    sign = jnp.where(mirrored == 1, -1.0, 1.0).astype(F32)
    up_ref[...] = jnp.zeros(up_ref.shape, F32)
    pack_ref[...] = jnp.zeros(pack_ref.shape, F32)
    edge = own_ref[:, oriented(mirrored, ROWS - 1 if first else 0)]

    def fetch(j, carried):
        at = oriented(mirrored, j)
        halo = halos[0][:, at]
        for k, ref in enumerate(halos[1:], 1):
            halo = jnp.where(choice == k, ref[:, at], halo)
        halo = jnp.where(outside == 1, edge, halo)
        x_ref[:, j] = own_ref[:, at] if first else halo
        x_ref[:, ROWS + j] = halo if first else own_ref[:, at]
        return carried

    lax.fori_loop(0, ROWS, fetch, 0, unroll=4)
    lane, sub = lanes((ny, nz)), sublanes((ny, nz))

    def load(i):
        return [x_ref[c, i] for c in range(COMPS)]

    def along(q, v, pressure):
        normal = sign * v[0]
        return [
            sign * q[1], q[1] * normal + sign * pressure, q[2] * normal, q[3] * normal, (q[4] + pressure) * normal
        ]

    def row(i, carried):
        q, v, pressure, sound, face_low = carried
        qn = load(i + 1)
        vn, pn, sn = primitives(qn)
        face_high = face(q, along(q, v, pressure), jnp.abs(v[0]) + sound, qn, along(qn, vn, pn), jnp.abs(vn[0]) + sn)
        total = [face_low[c] - face_high[c] for c in range(COMPS)]
        f = flux(q, v[1], pressure, 1)
        speed = jnp.abs(v[1]) + sound

        def below(a):
            return jnp.where(sub == 0, a, pltpu.roll(a, 1, 0))

        qb = [below(a) for a in q]
        fb = flux(qb, below(v[1]), below(pressure), 1)
        low = face(qb, fb, below(speed), q, f, speed)
        for c in range(COMPS):
            high = jnp.where(sub == ny - 1, 2.0 * f[c], pltpu.roll(low[c], ny - 1, 0))
            total[c] = total[c] + (low[c] - high)
        f = flux(q, v[2], pressure, 2)
        speed = jnp.abs(v[2]) + sound
        qb = [lane_roll(a, 1) for a in q]
        fb = flux(qb, lane_roll(v[2], 1), lane_roll(pressure, 1), 2)
        low = face(qb, fb, lane_roll(speed, 1), q, f, speed)
        rate = (
            jnp.abs(v[0]) + sound + (jnp.abs(v[1]) + sound) + (jnp.abs(v[2]) + sound) * refinement
        )
        scale = (0.5 * COURANT) / rate
        r = i - 1
        slot = lax.rem(r, 8)
        in_slot = ((lane >= slot * 7) & (lane < slot * 7 + 7)) | ((lane >= slot * 7 + 71) & (lane < slot * 7 + 78))
        picked = (lane == lax.rem(2 * r + nz - 1, nz)) | (lane == 2 * r) | (lane == 2 * r + 31) | (lane == 2 * r + 96)
        for c in range(COMPS):
            inner = jnp.where(lane == 0, 0.0, low[c])
            difference = inner - lane_roll(inner, nz - 1)
            value = (total[c] + refinement * difference) * scale
            res_ref[c, r] = value
            strip = lane_roll(value, lax.rem(slot * 7 + (nz - 25), nz))
            place = up_ref.at[c * groups + r // 8]
            place[...] = jnp.where(in_slot, strip, place[...])
            pack_ref[c] = jnp.where(picked, lane_roll(q[c], 2 * r), pack_ref[c])
        return qn, vn, pn, sn, face_high

    q0, q1 = load(0), load(1)
    v0, p0, s0 = primitives(q0)
    v1, p1, s1 = primitives(q1)
    low = face(q0, along(q0, v0, p0), jnp.abs(v0[0]) + s0, q1, along(q1, v1, p1), jnp.abs(v1[0]) + s1)
    lax.fori_loop(1, n + 1, row, (q1, v1, p1, s1, low), unroll=UNROLL)
    odd = lax.rem(lane, 2) == 1
    width, each, tiles = end_layout(n)
    ends, planes = [None] * tiles, [None] * tiles
    for c in range(COMPS):
        pack = pack_ref[c]
        plane = jnp.where(odd, lane_roll(pack, 31), lane_roll(pack, 97))
        k, shift = c // each, width * (c % each)
        if shift == 0:
            ends[k], planes[k] = pack, plane
        else:
            here = (lane >= shift - 1) & (lane < shift + width - 1)
            ends[k] = jnp.where(here, lane_roll(pack, shift), ends[k])
            planes[k] = jnp.where(here, lane_roll(plane, shift), planes[k])
    for k in range(tiles):
        down_ref[COMPS * half + k] = ends[k]
        up_ref[COMPS * groups + k] = planes[k]
    to_pair = jnp.concatenate([pairing(nz, nz // 4), pairing(nz, 3 * nz // 4)], axis=0)
    for c in range(COMPS):
        a = res_ref[c, :half].reshape(half * ny, nz)
        b = res_ref[c, half:].reshape(half * ny, nz)
        packed = split_dot(jnp.concatenate([a, b], axis=1), to_pair)
        down_ref[c * half : (c + 1) * half] = packed.reshape(half, ny, nz)
    if not first:
        odd_level = lax.rem(level, 2) == 1
        to_odd = (far_ref, near_chip_ref)
        for is_odd in (True, False):
            up_to, down_to = to_odd if is_odd else to_odd[::-1]

            @pl.when(odd_level if is_odd else jnp.logical_not(odd_level))
            def _(up_to=up_to, down_to=down_to):
                up_to[: up_ref.shape[0]] = up_ref[...]
                up_to[up_ref.shape[0] :] = jnp.zeros((up_to.shape[0] - up_ref.shape[0], ny, nz), F32)
                down_to[...] = down_ref[...]


def residuals(n, own, *halos):
    ny, nz = own.shape[2:]
    first = n == EARLY
    half, groups = n // 2, -(-n // 8)
    ends = end_layout(n)[2]
    down, up = COMPS * half + ends, COMPS * groups + ends
    tiles = (down, FIRST_UP_TILES) if first else (down, up, down, down)
    shapes = [(COMPS, n, ny, nz)] + [(k, ny, nz) for k in tiles]
    scratch = [pltpu.VMEM((COMPS, 2 * ROWS, ny, nz), F32), pltpu.VMEM((COMPS, ny, nz), F32)]
    vmem = pl.BlockSpec(memory_space=pltpu.VMEM)
    return pl.pallas_call(
        functools.partial(residual_kernel, n),
        out_shape=tuple(jax.ShapeDtypeStruct(k, F32) for k in shapes),
        in_specs=[vmem] * (1 + len(halos)),
        out_specs=(vmem,) * len(shapes),
        scratch_shapes=scratch,
        compiler_params=pltpu.CompilerParams(vmem_limit_bytes=8 * 2**20),
        cost_estimate=pl.CostEstimate(flops=2_000_000, bytes_accessed=2_000_000, transcendentals=0),
        name="residual_first" if first else "residual_second",
    )(own, *halos)


def end_faces(n, ends, planes, refinement):
    shape = ends[0].shape
    upper = lax.rem(lanes(shape), 2) == 1

    def parts(pack):
        width, each, _ = end_layout(n)
        return [lane_roll(pack[c // each], 128 - width * (c % each)) if c % each else pack[c // each] for c in range(COMPS)]

    q, g = parts(ends), parts(planes)
    v, pressure, sound = primitives(q)
    vg, pg, sg = primitives(g)
    f, fg = flux(q, v[2], pressure, 2), flux(g, vg[2], pg, 2)
    speed = jnp.maximum(jnp.abs(v[2]) + sound, jnp.abs(vg[2]) + sg)
    rate = jnp.abs(v[0]) + sound + (jnp.abs(v[1]) + sound) + (jnp.abs(v[2]) + sound) * refinement
    scale = (0.5 * COURANT) * refinement / rate
    out = []
    for c in range(COMPS):
        jump = speed * (q[c] - g[c])
        mean = f[c] + fg[c]
        out.append(jnp.where(upper, -(mean + jump), mean - jump) * scale)
    return out


def end_terms(n, flags, down_own, up_own, down_got, up_got, own_ref, finer_ref):
    level, refinement, top = flags
    tiles = end_layout(n)[2]
    half, groups = n // 2, -(-n // 8)
    ends = [down_own[COMPS * half + k] for k in range(tiles)]
    planes = [up_own[COMPS * groups + k] for k in range(tiles)]
    ends_finer = [jnp.where(top == 1, ends[k], down_got[COMPS * half + k]) for k in range(tiles)]
    planes_coarser = [jnp.where(level == 0, ends[k], up_got[COMPS * groups + k]) for k in range(tiles)]
    lane = lanes(ends[0].shape)
    near = (lane < 30) | (lane == lane.shape[-1] - 1)

    def halves(a):
        return 0.5 * jnp.where(lane < 64, lane_roll(a, 32), lane_roll(a, 96))

    for c, a in enumerate(end_faces(n, ends, planes_coarser, refinement)):
        own_ref[c] = jnp.where(near, a, halves(a))
    for c, a in enumerate(end_faces(n, ends_finer, planes, 2.0 * refinement)):
        finer_ref[c] = halves(a)


def sweep_kernel(
    n, w_ref, factor_ref, res, down_own, up_own, *refs
):
    first = n == EARLY
    if first:
        down_got, up_got, part_ref, t_ref, lhs_ref, own_ends, finer_ends = refs
    else:
        got_far, got_near_chip, u_ref, earlier_ref, out_ref, t_ref, lhs_ref, own_ends, finer_ends, down_got, up_got = refs
    level, block, refinement = axis_flags()
    top = (level == lax.axis_size("level") - 1).astype(jnp.int32)
    mirrored, _, first_outside, second_outside = orientation()
    keep_low = (second_outside == 0).astype(F32)
    keep_high = (first_outside == 0).astype(F32)
    ny, nz = t_ref.shape[2:]
    half, groups = n // 2, -(-n // 8)
    total = 2 * HALO + ROWS
    offset = LATE if first else 0
    if not first:
        odd_level = lax.rem(level, 2) == 1
        for is_odd in (True, False):
            down_from, up_from = (got_far, got_near_chip) if is_odd else (got_near_chip, got_far)

            @pl.when(odd_level if is_odd else jnp.logical_not(odd_level))
            def _(down_from=down_from, up_from=up_from):
                down_got[...] = down_from[...]
                up_got[...] = up_from[: up_got.shape[0]]

    end_terms(n, (level, refinement, top), down_own, up_own, down_got, up_got, own_ends, finer_ends)

    lane = lanes((ny, nz))
    covered = (lane >= 32) & (lane < 96)
    replaced = covered & (jnp.full((ny, nz), top, jnp.int32) == 0)
    outer = (lane == 0) | (lane == nz - 1)
    brink = (lane == 32) | (lane == 95)
    share = 1.0 / (1.0 + 6.0 * SMOOTHING)
    h = ny // 2
    sub1 = sublanes((h, nz))
    factor = factor_ref[...]
    weights = [SMOOTHING * share * k for k in (keep_low, 1.0, keep_high)]
    has_coarser = (level > 0).astype(F32)

    def zone(i):
        return 0 if i < HALO else 1 if i < HALO + ROWS else 2

    def add(terms):
        out = terms[0]
        for term in terms[1:]:
            out = out + term
        return out

    def smooth(which):
        def target(i):
            return tuple(t_ref[which, i, pl.ds(k, h, stride=2)] for k in range(2))

        rows = {offset + r: target(offset + r) for r in range(n)}
        for s in range(2, SWEEPS + 1):
            fresh = {}
            for i in range(s - 1, total - s + 1):
                if i in rows:
                    even, odd = rows[i]
                    n_even = odd + jnp.where(sub1 == 0, 0.0, pltpu.roll(odd, 1, 0))
                    n_odd = even + jnp.where(sub1 == h - 1, 0.0, pltpu.roll(even, h - 1, 0))
                    around = [(n_even + factor * even, n_odd + factor * odd)]
                else:
                    around = []
                beside = [rows[k] for k in (i - 1, i + 1) if k in rows]
                if not around and not beside:
                    continue
                w = weights[zone(i)]
                new = [w * add([a[k] for a in around + beside]) for k in range(2)]
                if offset <= i < offset + n:
                    new = [a + b for a, b in zip(target(i), new)]
                fresh[i] = tuple(new)
            rows = fresh
        return [rows[HALO + j] for j in range(ROWS)]

    def component(c, carried):
        own_c, finer_c = own_ends[c], finer_ends[c]
        for r in range(n):
            i = offset + r
            scale = share * (keep_low, 1.0, keep_high)[zone(i)]
            average = down_own[c * half + r % half]
            got = down_got[c * half + r % half]
            if r >= half:
                average, got = lane_roll(average, 64), lane_roll(got, 64)
            back = (nz - 2 * r) % nz
            term = lane_roll(own_c, back) if back else own_c
            term_finer = lane_roll(finer_c, back) if back else finer_c
            mine = res[c, r] + jnp.where(outer, term, 0.0)
            got = got + jnp.where(brink, term_finer, 0.0)
            lhs_ref[r * ny : (r + 1) * ny] = halved(jnp.where(replaced, got, mine) * scale)
            inside = average + jnp.where(brink, term, 0.0)
            shift = (25 - 7 * (r % 8)) % nz
            strip = lane_roll(up_got[c * groups + r // 8], shift)
            lhs_ref[(n + r) * ny : (n + r + 1) * ny] = halved(jnp.where(covered, inside, strip) * scale)
        t_ref[:, offset : offset + n] = transformed(lhs_ref[...], w_ref[0]).reshape(2, n, ny, nz)
        fine, coarse = smooth(0), smooth(1)
        if first:
            for j in range(ROWS):
                for k in range(2):
                    part_ref[c, j, k * h : (k + 1) * h] = fine[j][k]
                    part_ref[COMPS + c, j, k * h : (k + 1) * h] = coarse[j][k]
            return carried
        for which, swept in enumerate((fine, coarse)):
            for j in range(ROWS):
                for k in range(2):
                    before = earlier_ref[which * COMPS + c, j, k * h : (k + 1) * h]
                    t_ref[which, j, pl.ds(k, h, stride=2)] = swept[j][k] + before
                at = which * ROWS + j
                lhs_ref[at * ny : (at + 1) * ny] = halved(t_ref[which, j])
        own = transformed(lhs_ref[: ROWS * ny], w_ref[0]).reshape(ROWS, ny, nz)
        lifted = transformed(lhs_ref[ROWS * ny : 2 * ROWS * ny], w_ref[1]).reshape(ROWS, ny, nz)
        for j in range(ROWS):
            at = oriented(mirrored, j)
            out_ref[c, at] = u_ref[c, at] + (own[j] + lifted[j] * has_coarser)
        return carried

    lax.fori_loop(0, COMPS, component, 0, unroll=COMPS)


def sweeps(n, shape, *args):
    ny, nz = shape[2:]
    first = n == EARLY
    half, groups = n // 2, -(-n // 8)
    ends = pltpu.VMEM((COMPS, ny, nz), F32)
    out = (2 * COMPS, ROWS, ny, nz) if first else shape
    return pl.pallas_call(
        functools.partial(sweep_kernel, n),
        out_shape=jax.ShapeDtypeStruct(out, F32),
        in_specs=[pl.BlockSpec(memory_space=pltpu.VMEM)] * (1 + len(args)),
        out_specs=pl.BlockSpec(memory_space=pltpu.VMEM),
        scratch_shapes=[
            pltpu.VMEM((2, 2 * HALO + ROWS, ny, nz), F32), pltpu.VMEM((2 * n * ny, 2 * nz), jnp.bfloat16), ends, ends
        ]
        + ([] if first else [pltpu.VMEM((k, ny, nz), F32) for k in (COMPS * half + end_layout(n)[2], COMPS * groups + end_layout(n)[2])]),
        compiler_params=pltpu.CompilerParams(vmem_limit_bytes=16 * 2**20),
        cost_estimate=pl.CostEstimate(flops=10000000000, bytes_accessed=100000000, transcendentals=0),
        name="sweeps_first" if first else "sweeps_second",
    )(transforms(nz), *args)


def factors(nz):
    def kernel(out_ref):
        out_ref[...] = 2.0 * jnp.cos((np.pi / (nz + 1)) * (lanes((8, nz)) + 1).astype(F32))

    return pl.pallas_call(
        kernel,
        out_shape=jax.ShapeDtypeStruct((8, nz), F32),
        out_specs=pl.BlockSpec(memory_space=pltpu.VMEM),
        compiler_params=pltpu.CompilerParams(vmem_limit_bytes=2 * 2**20),
        cost_estimate=pl.CostEstimate(flops=10000000000, bytes_accessed=100000000, transcendentals=0),
        name="factors",
    )()


def shards(flow_state):
    fields = flow_state[0]
    ny, nz = fields.shape[2:]
    levels, blocks = lax.axis_size("level"), lax.axis_size("block")
    inner = [i for i in range(blocks - 1) if i % LINE != LINE - 1]
    ends = [i for i in range(blocks - 1) if i % LINE == LINE - 1]
    rise = [(i, i + 1) for i in inner]
    fall = [(i + 1, i) for i in inner if i % LINE != LINE - 2]
    last = [(i + 1, i) for i in inner if i % LINE == LINE - 2]
    swap = [(i, i + 1) for i in ends] + [(i + 1, i) for i in ends]
    finer = [(i, i + 1) for i in range(levels - 1)]
    coarser = [(i + 1, i) for i in range(levels - 1)]
    across = [(i, i + 1) for i in range(1, levels - 1, 2)] + [(i + 1, i) for i in range(1, levels - 1, 2)]
    within = [(i, i + 1) for i in range(0, levels - 1, 2)] + [(i + 1, i) for i in range(0, levels - 1, 2)]
    above = lax.ppermute(fields, "block", fall)
    below = lax.ppermute(fields, "block", rise)
    sent, factor = lax.optimization_barrier((fields, factors(nz)))
    beyond = lax.ppermute(sent, "block", swap)
    res1, down1, up1 = residuals(EARLY, fields, above, below)
    got_down1 = lax.ppermute(down1, "level", coarser)
    got_up1 = lax.ppermute(up1, "level", finer)
    own, down1 = lax.optimization_barrier((fields, down1))
    edge = lax.ppermute(own, "block", last)
    res0, down0, up0, far0, near0 = residuals(LATE, own, below, beyond, edge)
    got_far0 = lax.ppermute(far0, "level", across)
    got_near0 = lax.ppermute(near0, "level", within)
    res1, res0 = lax.optimization_barrier((res1, res0))
    part = sweeps(EARLY, fields.shape, factor, res1, down1, up1, got_down1, got_up1)
    out = sweeps(LATE, fields.shape, factor, res0, down0, up0, got_far0, got_near0, own, part)
    return out[None]


def solution(mesh):
    spec = P("level", None, "block", None, None)
    return jax.shard_map(shards, mesh=mesh, in_specs=(spec,), out_specs=spec, check_vma=False)
```
